128 devices in a mesh: row: 16 (over z_lo, y, core), col: 8 (over z_hi, x).
Axes of the slice: x: 4, y: 4, z: 4 (z_hi: 2, z_lo: 2; z = z_hi * 2 + z_lo), core: 2. Of those that a mesh axis runs over, the one named last changes fastest.
Arguments:
- iterate: bfloat16 [6144, 9216], P('row', 'col'), may hold values from -2.1875 to 2.1875
Outputs:
- update: bfloat16 [6144, 9216], P('row', 'col')
The draws below stay inside these ranges and needn't reach their ends.
All inputs are finite; a program needn't handle non-finite values.
Results may differ from the reference program's by a relative error of at most 0.0052.
Values may be sent and summed in bfloat16 or wider, within the bound.
No kernel may reach another device: no remote copies, remote signals or barrier semaphores. Data moves between devices by JAX's collectives and lax.ppermute only.
A program may use at most 128 MiB of HBM per device.

```python
import jax
import jax.numpy as jnp
from jax import lax

M = 6144
N = 9216


def draw_iterate(key, part):
    key = jax.random.fold_in(key, 7)
    base_key = jax.random.fold_in(key, 0)
    values = 0.55 * jax.random.normal(base_key, (M, N), jnp.float32)
    return jnp.clip(values, -2.1875, 2.1875).astype(jnp.bfloat16)


def setup_inputs(seed: int = 0) -> dict:
    splits = jax.random.split(jax.random.key(seed), 2)
    iterate = draw_iterate(jax.random.fold_in(splits[1], 71), 0)
    return dict(iterate=iterate)


lead_coef = 3.4445
square_coef = -4.7750
quart_coef = 2.0315


def reference(iterate):
    values = iterate.astype(jnp.float32)
    gram = (jnp.dot(values, values.T, precision=lax.Precision.HIGHEST) / N).astype(jnp.bfloat16)
    gram_wide = gram.astype(jnp.float32)
    square = jnp.dot(gram_wide, gram_wide, precision=lax.Precision.HIGHEST)
    poly = (square_coef * gram_wide + quart_coef * square).astype(jnp.bfloat16)
    mixed = jnp.dot(poly.astype(jnp.float32), values, precision=lax.Precision.HIGHEST)
    return (lead_coef * values + mixed).astype(jnp.bfloat16)
```

```python
import jax
import jax.numpy as jnp
from jax import lax
from jax.sharding import Mesh, PartitionSpec as P

N = 9216

lead_coef = 3.4445
square_coef = -4.775
quart_coef = 2.0315

AXES = ("zl", "y", "c", "zh", "x")
SIZES = (2, 4, 2, 2, 4)
ROW = ("zl", "y", "c")
COL = ("zh", "x")
f32 = jnp.float32
bf16 = jnp.bfloat16


def shift(axis, by):
    size = SIZES[AXES.index(axis)]
    pairs = [(i, (i + by) % size) for i in range(size)]
    return lambda v: lax.ppermute(v, axis, pairs)


swap_zl = shift("zl", 1)
swap_core = shift("c", 1)
up = shift("y", 1)
down = shift("y", -1)


def cat(*parts):
    return jnp.concatenate(parts, axis=0)


def gather_x(own):
    t = own.shape[0] // 3
    h = t // 2
    from_m = up(own)
    from_p = down(own)
    z0 = swap_zl(own[: 2 * t])
    batches = [[own]]
    batches.append([z0])
    batches.append([from_m, from_p])
    two_m = up(cat(from_m[:t], from_m[2 * t : 2 * t + h]))
    two_p = down(cat(from_p[t : 2 * t], from_p[2 * t + h :]))
    z0_m = up(z0)
    z0_p = down(z0)
    z1 = swap_zl(cat(own[2 * t :], from_m[2 * t :], from_p[2 * t :]))
    batches.append([two_m, two_p, z0_m, z0_p])
    z0_2m = up(z0_m[:t])
    z0_2p = down(z0_p[t:])
    z1_2 = swap_zl(cat(two_m[t:], two_p[t:]))
    batches.append([z1])
    batches.append([z0_2m, z0_2p, z1_2])
    out = []
    for parts in batches:
        mine = cat(*parts) if len(parts) > 1 else parts[0]
        out.append(cat(mine, swap_core(mine)))
    return out


def places():
    at = {}
    at[0, 0] = [(0, 0, 2), (0, 2, 2), (0, 4, 2)]
    at[0, 1] = [(2, 0, 2), (2, 2, 2), (2, 4, 2)]
    at[0, 3] = [(2, 6, 2), (2, 8, 2), (2, 10, 2)]
    at[0, 2] = [(3, 0, 2), (3, 3, 2), [(3, 2, 1), (3, 5, 1)]]
    at[1, 0] = [(1, 0, 2), (1, 2, 2), (4, 0, 2)]
    at[1, 1] = [(3, 6, 2), (3, 8, 2), (4, 2, 2)]
    at[1, 3] = [(3, 10, 2), (3, 12, 2), (4, 4, 2)]
    at[1, 2] = [(5, 0, 2), (5, 2, 2), (5, 4, 2)]
    return at


def block_rows(panels, dz, dy, third, core, h):
    spec = places()[dz, dy][third]
    spec = spec if isinstance(spec, list) else [spec]
    parts = []
    for batch, first, count in spec:
        panel = panels[batch]
        base = core * (panel.shape[0] // 2)
        parts.append(panel[base + first * h : base + (first + count) * h])
    return parts


def reduce_x(terms):
    rows, cols = terms.shape
    got = lax.all_to_all(terms, "x", 0, 0, tiled=True)
    part = got.reshape(4, rows // 4, cols).astype(f32).sum(0).astype(bf16)
    got = lax.all_to_all(part, "zh", 0, 0, tiled=True)
    return got.reshape(2, rows // 8, cols).astype(f32).sum(0)


def spread_x(slices):
    rows, cols = slices.shape
    pair = lax.all_to_all(jnp.broadcast_to(slices[None], (2, rows, cols)), "zh", 0, 0, tiled=True)
    return lax.all_to_all(jnp.broadcast_to(pair[None], (4, 2, rows, cols)), "x", 0, 0, tiled=True)


def gather_y_late(v):
    t = v.shape[0]
    h = t // 2
    m = up(v)
    p = down(v)
    z_a = swap_zl(cat(v, m, p))
    m2 = up(m[:h])
    p2 = down(p[h:])
    z_b = swap_zl(cat(m2, p2))
    first = cat(v, m, p, z_a)
    second = cat(m2, p2, z_b)
    return [(first, [(0, 0), (0, 1), (0, 3), (1, 0), (1, 1), (1, 3)]), (second, [(0, 2), (1, 2)])]


def gather_y_early(v):
    t = v.shape[0]
    z = swap_zl(v)
    pair = cat(v, z)
    m = up(pair)
    p = down(pair)
    m2 = up(m[:t])
    p2 = down(p[t:])
    first = cat(pair, m, p)
    second = cat(m2, p2)
    return [(first, [(0, 0), (1, 0), (0, 1), (1, 1), (0, 3), (1, 3)]), (second, [(0, 2), (1, 2)])]


def tdot(a, b):
    return lax.dot_general(a, b, (((0,), (0,)), ((), ())), preferred_element_type=f32)


def local(own):
    rows = own.shape[0]
    t = rows // 3
    h = t // 2
    batches = gather_x(own)
    slices = []
    for b in batches:
        terms = lax.dot_general(b, own, (((1,), (1,)), ((), ())), preferred_element_type=f32)
        slices.append((reduce_x(terms.astype(bf16)) / N).astype(bf16))
    slices = cat(*slices)
    sizes = [b.shape[0] // 8 for b in batches]
    gram = []
    ys = []
    mixed = jnp.zeros(own.shape, f32)
    pieces = []
    for k in range(3):
        full = spread_x(slices[:, k * t : (k + 1) * t])
        panels = []
        first = 0
        for size in sizes:
            panels.append(full[:, :, first : first + size].reshape(8 * size, t))
            first += size
        gram.append(panels)
        y = sum(tdot(g, b) for g, b in zip(panels, batches))
        ys.append(y)
        y16 = y.astype(bf16)
        pieces.append(gather_y_late(y16) if k == 0 else gather_y_early(y16))
    wide = [jnp.concatenate([gram[k][i] for k in range(3)], axis=1) for i in range(len(batches))]
    for k in range(3):
        for part, keys in pieces[k]:
            both = cat(part, swap_core(part))
            g = []
            for core in range(2):
                for dz, dy in keys:
                    g += block_rows(wide, dz, dy, k, core, h)
            mixed = mixed + tdot(cat(*g), both)
    return (lead_coef * own.astype(f32) + square_coef * cat(*ys) + quart_coef * mixed).astype(bf16)


def solution(mesh):
    fine = Mesh(mesh.devices.reshape(SIZES), AXES)
    spec = P(ROW, COL)
    return jax.shard_map(local, mesh=fine, in_specs=(spec,), out_specs=spec, check_vma=False)
```

```python
import jax
import jax.numpy as jnp
from jax import lax
from jax.sharding import Mesh, PartitionSpec as P

N = 9216

lead_coef = 3.4445
square_coef = -4.775
quart_coef = 2.0315

AXES = ("zl", "y", "c", "zh", "x")
SIZES = (2, 4, 2, 2, 4)
ROW = ("zl", "y", "c")
COL = ("zh", "x")
f32 = jnp.float32
bf16 = jnp.bfloat16

SIBLING = {"v": "w", "r0": "o0", "r1": "o1", "f": "g"}


def swap_zl(v):
    return lax.ppermute(v, "zl", [(0, 1), (1, 0)])


def swap_zh(v):
    return lax.ppermute(v, "zh", [(0, 1), (1, 0)])


def swap_core(v):
    return lax.ppermute(v, "c", [(0, 1), (1, 0)])


def along_y(v):
    pairs = []
    for y in range(4):
        pairs.append((y * 2, (y + 1) % 4 * 2))
        pairs.append((y * 2 + 1, (y - 1) % 4 * 2 + 1))
    return lax.ppermute(v, ("y", "c"), pairs)


def cat(*parts):
    return jnp.concatenate(parts, axis=0) if len(parts) > 1 else parts[0]


def sib(keys):
    return [(plane, SIBLING[slot], third) for plane, slot, third in keys]


def blocks(plane, slots, thirds):
    return [(plane, slot, third) for slot in slots for third in thirds]


def gather_x(own):
    t = own.shape[0] // 3
    w = swap_core(own)
    z = swap_zl(own[: 2 * t])
    r = along_y(cat(own, w))
    zw = swap_core(z)
    rz = along_y(cat(z, zw))
    o = swap_core(r)
    f = along_y(r[: 3 * t])
    zr = swap_zl(cat(own[2 * t :], r[2 * t : 3 * t], r[5 * t :]))
    g = swap_core(f)
    oz = swap_core(rz)
    fz = along_y(rz[: 2 * t])
    zf = swap_zl(f[2 * t :])
    szr = swap_core(zr)
    end = cat(fz, zf)
    send = swap_core(end)
    k_v = blocks(0, ["v"], range(3))
    k_z = blocks(1, ["v"], range(2))
    k_r = blocks(0, ["r0", "r1"], range(3))
    k_rz = blocks(1, ["r0", "r1"], range(2))
    k_f = blocks(0, ["f"], range(3))
    k_zr = blocks(1, ["v", "r0", "r1"], [2])
    k_end = blocks(1, ["f"], range(3))
    return [
        [(own, k_v), (w, sib(k_v)), (z, k_z), (zw, sib(k_z))],
        [(r, k_r), (o, sib(k_r))],
        [(f, k_f), (g, sib(k_f)), (rz, k_rz), (oz, sib(k_rz)), (zr, k_zr), (szr, sib(k_zr))],
        [(end, k_end), (send, sib(k_end))],
    ]


def gather_late(v, k):
    t = v.shape[0]
    w = swap_core(v)
    r = along_y(cat(v, w))
    o = swap_core(r)
    za = swap_zl(cat(v, r))
    f = along_y(r[:t])
    g = swap_core(f)
    zb = swap_zl(f)
    sza = swap_core(za)
    szb = swap_core(zb)
    return [
        ([v, w, r, o], blocks(0, ["v", "w", "r0", "r1", "o0", "o1"], [k])),
        ([za, sza], blocks(1, ["v", "r0", "r1", "w", "o0", "o1"], [k])),
        ([f, g, zb, szb], blocks(0, ["f", "g"], [k]) + blocks(1, ["f", "g"], [k])),
    ]


def gather_early(v, k):
    t = v.shape[0]
    pair = cat(v, swap_zl(v))
    chip = cat(pair, swap_core(pair))
    r = along_y(chip)
    o = swap_core(r)
    f = along_y(r[: 2 * t])
    g = swap_core(f)
    both = lambda slot: [(0, slot, k), (1, slot, k)]
    return [
        ([chip], both("v") + both("w")),
        ([r, o], both("r0") + both("r1") + both("o0") + both("o1")),
        ([f, g], both("f") + both("g")),
    ]


def ordered(mine, other):
    first = lax.axis_index("zh") == 0
    return jnp.stack([jnp.where(first, mine, other), jnp.where(first, other, mine)])


def reduce_zh(part):
    me = lax.axis_index("zh")
    keep = lax.dynamic_index_in_dim(part, me, 0, keepdims=False)
    give = lax.dynamic_index_in_dim(part, 1 - me, 0, keepdims=False)
    return keep.astype(f32) + swap_zh(give).astype(f32)


def tdot(a, b):
    return lax.dot_general(a, b, (((0,), (0,)), ((), ())), preferred_element_type=f32)


def local(own):
    rows = own.shape[0]
    t = rows // 3
    batches = gather_x(own)
    parts = []
    for batch in batches:
        terms = []
        for piece, _ in batch:
            term = lax.dot_general(piece, own, (((1,), (1,)), ((), ())), preferred_element_type=f32)
            terms.append(term.astype(bf16).reshape(8, -1, rows))
        terms = jnp.concatenate(terms, axis=1) if len(terms) > 1 else terms[0]
        size = terms.shape[1]
        got = lax.all_to_all(terms.reshape(8 * size, rows), "x", 0, 0, tiled=True)
        parts.append(got.reshape(4, 2, size, rows).astype(f32).sum(0).astype(bf16))
    slices = []
    for pair in (parts[:2], parts[2:]):
        slices.append((reduce_zh(jnp.concatenate(pair, axis=1)) / N).astype(bf16))
    slices = cat(*slices)

    gram = []
    ys = []
    pieces = []
    for k in range(3):
        mine = slices[:, k * t : (k + 1) * t]
        pair = ordered(mine, swap_zh(mine))
        full = lax.all_to_all(jnp.broadcast_to(pair[None], (4,) + pair.shape), "x", 0, 0, tiled=True)
        where = {}
        y = 0.0
        first = 0
        for batch in batches:
            for piece, keys in batch:
                size = piece.shape[0] // 8
                g = full[:, :, first : first + size].reshape(8 * size, t)
                first += size
                y = y + tdot(g, piece)
                for i, key in enumerate(keys):
                    where[key] = g[i * t : (i + 1) * t]
        gram.append(where)
        ys.append(y)
        y16 = y.astype(bf16)
        pieces.append(gather_late(y16, k) if k == 0 else gather_early(y16, k))
    mixed = 0.0
    for groups in pieces:
        for part, keys in groups:
            g = jnp.concatenate([cat(*[gram[k][key] for key in keys]) for k in range(3)], axis=1)
            mixed = mixed + tdot(g, cat(*part))
    return (lead_coef * own.astype(f32) + square_coef * cat(*ys) + quart_coef * mixed).astype(bf16)


def solution(mesh):
    fine = Mesh(mesh.devices.reshape(SIZES), AXES)
    spec = P(ROW, COL)
    return jax.shard_map(local, mesh=fine, in_specs=(spec,), out_specs=spec, check_vma=False)
```

```python
import jax
import jax.numpy as jnp
from jax import lax
from jax.experimental import pallas as pl
from jax.experimental.pallas import tpu as pltpu
from jax.sharding import Mesh, PartitionSpec as P

N = 9216

lead_coef = 3.4445
square_coef = -4.775
quart_coef = 2.0315

AXES = ("zl", "y", "c", "zh", "x")
SIZES = (2, 4, 2, 2, 4)
ROW = ("zl", "y", "c")
COL = ("zh", "x")
f32 = jnp.float32
bf16 = jnp.bfloat16
VMEM_LIMIT = 40 * 2**20

SIBLING = {"v": "w", "r0": "o0", "r1": "o1", "f": "g"}


def swap_zl(v):
    return lax.ppermute(v, "zl", [(0, 1), (1, 0)])


def swap_zh(v):
    return lax.ppermute(v, "zh", [(0, 1), (1, 0)])


def swap_core(v):
    return lax.ppermute(v, "c", [(0, 1), (1, 0)])


def along_y(v):
    pairs = []
    for y in range(4):
        pairs.append((y * 2, (y + 1) % 4 * 2))
        pairs.append((y * 2 + 1, (y - 1) % 4 * 2 + 1))
    return lax.ppermute(v, ("y", "c"), pairs)


def cat(*parts):
    return jnp.concatenate(parts, axis=0) if len(parts) > 1 else parts[0]


def after(value, *first):
    return lax.optimization_barrier((value,) + first)[0]


def sib(keys):
    return [(plane, SIBLING[slot], third) for plane, slot, third in keys]


def blocks(plane, slots, thirds):
    return [(plane, slot, third) for slot in slots for third in thirds]


def gather_x(own):
    t = own.shape[0] // 3
    w = swap_core(own)
    z = swap_zl(own[: 2 * t])
    r = along_y(cat(own, w))
    zw = swap_core(z)
    f = along_y(r[: 3 * t])
    o = swap_core(r)
    rz = along_y(after(cat(z, zw), f))
    zr = swap_zl(cat(own[2 * t :], r[2 * t : 3 * t], r[5 * t :]))
    g = swap_core(f)
    oz = swap_core(rz)
    fz = along_y(rz[: 2 * t])
    zf = swap_zl(f[2 * t :])
    szr = swap_core(zr)
    end = cat(fz, zf)
    send = swap_core(end)
    k_v = blocks(0, ["v"], range(3))
    k_z = blocks(1, ["v"], range(2))
    k_r = blocks(0, ["r0", "r1"], range(3))
    k_rz = blocks(1, ["r0", "r1"], range(2))
    k_f = blocks(0, ["f"], range(3))
    k_zr = blocks(1, ["v", "r0", "r1"], [2])
    k_end = blocks(1, ["f"], range(3))
    return [
        (own, k_v), (w, sib(k_v)), (z, k_z), (zw, sib(k_z)), (r, k_r), (o, sib(k_r)), (f, k_f), (g, sib(k_f)),
        (rz, k_rz), (oz, sib(k_rz)), (zr, k_zr), (szr, sib(k_zr)), (end, k_end), (send, sib(k_end)),
    ]


BATCHES = (2, 1, 2, 1)
STARTS = (0, 2, 3, 5)


def gather_late(v, k):
    t = v.shape[0]
    w = swap_core(v)
    r = along_y(cat(v, w))
    o = swap_core(r)
    za = swap_zl(cat(v, r))
    f = along_y(r[:t])
    g = swap_core(f)
    zb = swap_zl(f)
    sza = swap_core(za)
    szb = swap_core(zb)
    return [
        ([v, w, r, o], blocks(0, ["v", "w", "r0", "r1", "o0", "o1"], [k])),
        ([za, sza], blocks(1, ["v", "r0", "r1", "w", "o0", "o1"], [k])),
        ([f, g, zb, szb], blocks(0, ["f", "g"], [k]) + blocks(1, ["f", "g"], [k])),
    ]


def gather_early(v, k):
    t = v.shape[0]
    pair = cat(v, swap_zl(v))
    spair = swap_core(pair)
    r = along_y(cat(pair, spair))
    o = swap_core(r)
    f = along_y(r[: 2 * t])
    g = swap_core(f)
    both = lambda slot: [(0, slot, k), (1, slot, k)]
    return [
        ([pair, spair], both("v") + both("w")),
        ([r, o], both("r0") + both("r1") + both("o0") + both("o1")),
        ([f, g], both("f") + both("g")),
    ]


VM = pl.BlockSpec(memory_space=pltpu.VMEM)
SM = pl.BlockSpec(memory_space=pltpu.SMEM)
ANY = pl.BlockSpec(memory_space=pl.ANY)


def call(kernel, out_shape, in_specs, scratch, flops, moved, *args):
    outs = jax.tree.map(lambda _: VM, out_shape)
    return pl.pallas_call(
        kernel,
        out_shape=out_shape,
        in_specs=in_specs,
        out_specs=outs,
        scratch_shapes=scratch,
        cost_estimate=pl.CostEstimate(flops=flops, bytes_accessed=moved, transcendentals=0),
        compiler_params=pltpu.CompilerParams(vmem_limit_bytes=VMEM_LIMIT),
    )(*args)


def start_copies(copies, refs, panel, sems):
    started = []
    for i, (ref, src, dst, rows) in enumerate(copies):
        copy = pltpu.make_async_copy(refs[ref].at[pl.ds(src, rows)], panel.at[pl.ds(dst, rows)], sems.at[i])
        copy.start()
        started.append(copy)
    return started


def terms_of(zh, own, arrays, copies, size):
    rows, depth = own.shape
    total = 8 * size

    def kernel(zh_ref, own_ref, *refs):
        refs, out, panel, sems = refs[:-3], refs[-3], refs[-2], refs[-1]
        for copy in start_copies(copies, refs, panel, sems):
            copy.wait()
        me = zh_ref[0]
        for x in range(4):
            term = lax.dot_general(
                panel[2 * size * x : 2 * size * (x + 1)],
                own_ref[...],
                (((1,), (1,)), ((), ())),
                preferred_element_type=f32,
            ).astype(bf16)
            for h in range(2):
                out[x, lax.rem(me + h, 2)] = term[h * size : (h + 1) * size]

    return call(
        kernel,
        jax.ShapeDtypeStruct((4, 2, size, rows), bf16),
        [SM, VM] + [ANY] * len(arrays),
        [pltpu.VMEM((total, depth), bf16), pltpu.SemaphoreType.DMA((len(copies),))],
        2 * total * rows * depth,
        2 * total * (rows + depth),
        zh, own, *arrays,
    )


def sum_x(got):
    _, _, size, rows = got.shape

    def kernel(got_ref, keep, give):
        keep[...] = sum(got_ref[x, 0].astype(f32) for x in range(4))
        give[...] = sum(got_ref[x, 1].astype(f32) for x in range(4)).astype(bf16)

    out = [jax.ShapeDtypeStruct((size, rows), f32), jax.ShapeDtypeStruct((size, rows), bf16)]
    return call(kernel, out, [VM], [], 8 * size * rows, 22 * size * rows, got)


def finish(keeps, gots):
    rows = keeps[0].shape[1]
    t = rows // 3
    count = len(keeps)

    def kernel(*refs):
        outs = refs[2 * count :]
        first = 0
        for keep, got in zip(refs[:count], refs[count : 2 * count]):
            size = keep.shape[0]
            for b in range(size // t):
                part = pl.ds(b * t, t)
                value = (keep[part] + got[part].astype(f32)) / N
                for k in range(3):
                    outs[k][:, first + b * t : first + (b + 1) * t] = value[:, k * t : (k + 1) * t].T.astype(bf16)
            first += size

    out = [jax.ShapeDtypeStruct((t, 6 * t), bf16)] * 3
    return call(kernel, out, [VM] * (2 * count), [], 36 * t * t, 48 * t * t * 3, *keeps, *gots)


def spread(mine, other):
    def kernel(a, b, out):
        for x in range(4):
            out[x, 0] = a[...]
            out[x, 1] = b[...]

    out = jax.ShapeDtypeStruct((4, 2) + mine.shape, bf16)
    return call(kernel, out, [VM, VM], [], 0, 20 * mine.size, mine, other)


def times_x(zh, full, arrays, copies):
    _, _, t, depth = full.shape
    cols = arrays[0].shape[1]

    def kernel(zh_ref, full_ref, *refs):
        refs, (y, y16, gram), panel, sems = refs[:-5], refs[-5:-2], refs[-2], refs[-1]
        started = start_copies(copies, refs, panel, sems)
        me = zh_ref[0]
        total = None
        for e in range(8):
            for copy, spec in zip(started, copies):
                if spec[2] // depth == e:
                    copy.wait()
            g = full_ref[e // 2, lax.rem(me + e % 2, 2)]
            gram[e] = g
            part = jnp.dot(g, panel[e * depth : (e + 1) * depth], preferred_element_type=f32)
            if e == 0:
                y[...] = part
            elif e < 7:
                y[...] += part
            else:
                total = y[...] + part
        y[...] = total
        y16[...] = total.astype(bf16)

    out = [
        jax.ShapeDtypeStruct((t, cols), f32),
        jax.ShapeDtypeStruct((t, cols), bf16),
        jax.ShapeDtypeStruct((8, t, depth), bf16),
    ]
    return call(
        kernel, out, [SM, VM] + [ANY] * len(arrays),
        [pltpu.VMEM((8 * depth, cols), bf16), pltpu.SemaphoreType.DMA((len(copies),))],
        2 * 8 * depth * t * cols, 2 * 8 * depth * (t + cols), zh, full, *arrays,
    )


def times_y(grams, arrays, spots, total, last):
    _, t, depth = grams[0].shape
    cols = arrays[0].shape[1]
    copies = []
    for i, a in enumerate(arrays):
        copies.append((i, 0, sum(c[3] for c in copies), a.shape[0]))
    extra = ([total] if total is not None else []) + (list(last) if last else [])

    def kernel(*refs):
        gs = refs[:3]
        ex = refs[3 : 3 + len(extra)]
        ys = refs[3 + len(extra) : 3 + len(extra) + len(arrays)]
        out, panel, sems = refs[-3:]
        started = start_copies(copies, ys, panel, sems)
        for copy in started:
            copy.wait()
        for i in range(3):
            part = slice(i * t, (i + 1) * t)
            left = jnp.concatenate([gs[i][e, :, j * t : (j + 1) * t] for e, j in spots], axis=1)
            value = jnp.dot(left, panel[...], preferred_element_type=f32)
            if total is not None:
                value = ex[0][part] + value
            if last:
                own, thirds = ex[-4], ex[-3:]
                value = lead_coef * own[part].astype(f32) + square_coef * thirds[i][...] + quart_coef * value
            out[part] = value.astype(out.dtype)

    return call(
        kernel, jax.ShapeDtypeStruct((3 * t, cols), bf16 if last else f32),
        [VM] * (3 + len(extra)) + [ANY] * len(arrays),
        [pltpu.VMEM((len(spots) * t, cols), bf16), pltpu.SemaphoreType.DMA((len(copies),))],
        2 * 3 * t * len(spots) * t * cols, 2 * len(spots) * t * cols, *grams, *extra, *arrays,
    )


def local(own):
    rows = own.shape[0]
    t = rows // 3
    zh = lax.axis_index("zh").astype(jnp.int32).reshape(1)
    pieces = gather_x(own)

    queue = [(p, i * t, key) for p, (_, keys) in enumerate(pieces) for i, key in enumerate(keys)]
    keeps, gots = [], []
    place = {}
    panel_copies = []
    first = 0
    for b, per in enumerate(BATCHES):
        mine = queue[first : first + 8 * per]
        first += 8 * per
        used = sorted({p for p, _, _ in mine})
        copies = []
        for i, (p, row, key) in enumerate(mine):
            e, j = i // per, STARTS[b] + i % per
            place[key] = (e, j)
            panel_copies.append((p, row, (e * 6 + j) * t, t))
            if copies and copies[-1][0] == used.index(p):
                ref, src, dst, count = copies[-1]
                copies[-1] = (ref, src, dst, count + t)
            else:
                copies.append((used.index(p), row, i * t, t))
        terms = terms_of(zh, own, [pieces[p][0] for p in used], copies, per * t)
        got = lax.all_to_all(terms, "x", 0, 0, tiled=True)
        keep, give = sum_x(got)
        keeps.append(keep)
        gots.append(swap_zh(give))
    slices = finish(keeps, gots)
    panel_copies.sort(key=lambda c: c[2])
    arrays = [a for a, _ in pieces]

    grams, ys, groups = [], [], []
    full = None
    for k in range(3):
        mine = slices[k]
        sent = spread(mine, swap_zh(mine))
        if full is not None:
            sent = after(sent, full)
        full = lax.all_to_all(sent, "x", 0, 0, tiled=True)
        if k > 0:
            full = after(full, y16)
        y, y16, gram = times_x(zh, full, arrays, panel_copies)
        ys.append(y)
        grams.append(gram)
        groups += gather_late(y16, k) if k == 0 else gather_early(y16, k)
    total = None
    for i, (parts, keys) in enumerate(groups):
        last = [own] + ys if i == len(groups) - 1 else None
        total = times_y(grams, parts, [place[key] for key in keys], total, last)
    return total


def solution(mesh):
    fine = Mesh(mesh.devices.reshape(SIZES), AXES)
    spec = P(ROW, COL)
    return jax.shard_map(local, mesh=fine, in_specs=(spec,), out_specs=spec, check_vma=False)
```

```python
import jax
import jax.numpy as jnp
from jax import lax
from jax.experimental import pallas as pl
from jax.experimental.pallas import tpu as pltpu
from jax.sharding import Mesh, PartitionSpec as P

N = 9216

lead_coef = 3.4445
square_coef = -4.775
quart_coef = 2.0315

AXES = ("zl", "y", "c", "zh", "x")
SIZES = (2, 4, 2, 2, 4)
ROW = ("zl", "y", "c")
COL = ("zh", "x")
f32 = jnp.float32
bf16 = jnp.bfloat16
VMEM_LIMIT = 36 * 2**20

SIBLING = {"v": "w", "r0": "o0", "r1": "o1", "f": "g"}


def swap_zl(v):
    return lax.ppermute(v, "zl", [(0, 1), (1, 0)])


def swap_zh(v):
    return lax.ppermute(v, "zh", [(0, 1), (1, 0)])


def swap_core(v):
    return lax.ppermute(v, "c", [(0, 1), (1, 0)])


def swap_x1(v):
    return lax.ppermute(v, "x", [(i, i ^ 1) for i in range(4)])


def swap_x3(v):
    return lax.ppermute(v, "x", [(i, i ^ 3) for i in range(4)])


def partner(v, first):
    pairs = []
    for c in range(2):
        by = 1 if (c == 0) == first else 3
        pairs += [(c * 4 + x, c * 4 + (x ^ by)) for x in range(4)]
    return lax.ppermute(v, ("c", "x"), pairs)


def along_y(v):
    pairs = []
    for y in range(4):
        pairs.append((y * 2, (y + 1) % 4 * 2))
        pairs.append((y * 2 + 1, (y - 1) % 4 * 2 + 1))
    return lax.ppermute(v, ("y", "c"), pairs)


def cat(*parts):
    return jnp.concatenate(parts, axis=0) if len(parts) > 1 else parts[0]


def together(*values):
    return lax.optimization_barrier(values)


def sib(keys):
    return [(plane, SIBLING[slot], third) for plane, slot, third in keys]


def blocks(plane, slots, thirds):
    return [(plane, slot, third) for slot in slots for third in thirds]


BATCHES = (1, 2, 2, 1)
STARTS = (0, 1, 3, 5)
ARRIVAL = (
    (0, "v"), (0, "w"), (0, "r0"), (0, "o0"), (1, "v"), (0, "r1"), (1, "w"), (0, "o1"),
    (0, "f"), (0, "g"), (1, "r0"), (1, "o0"), (1, "r1"), (1, "f"), (1, "o1"), (1, "g"),
)


VM = pl.BlockSpec(memory_space=pltpu.VMEM)
SM = pl.BlockSpec(memory_space=pltpu.SMEM)
HBM = pl.BlockSpec(memory_space=pltpu.HBM)


def call(kernel, out_shape, in_specs, scratch, flops, moved, *args):
    outs = jax.tree.map(lambda _: VM, out_shape)
    return pl.pallas_call(
        kernel,
        out_shape=out_shape,
        in_specs=in_specs,
        out_specs=outs,
        scratch_shapes=scratch,
        cost_estimate=pl.CostEstimate(flops=flops, bytes_accessed=moved, transcendentals=0),
        compiler_params=pltpu.CompilerParams(vmem_limit_bytes=VMEM_LIMIT),
    )(*args)


def place_of(where_ref, d, h):
    return jnp.bitwise_xor(where_ref[0], d) * 2 + jnp.bitwise_xor(where_ref[1], h)


def start_copies(copies, refs, panel, sems):
    started = []
    for i, (ref, src, dst, rows) in enumerate(copies):
        copy = pltpu.make_async_copy(refs[ref].at[pl.ds(src, rows)], panel.at[pl.ds(dst, rows)], sems.at[i])
        copy.start()
        started.append(copy)
    return started


def terms_of(where, own, arrays, copies, size):
    rows, depth = own.shape
    total = 8 * size

    def kernel(where_ref, own_ref, *refs):
        refs, keep, send, panel, sems = refs[:-4], refs[-4], refs[-3], refs[-2], refs[-1]
        started = start_copies(copies, refs, panel, sems)
        for copy in started:
            copy.wait()
        first, second = where_ref[2], where_ref[3]
        for out, slot, d in ((send, 0, first), (send, 1, 2), (keep, 0, 0), (keep, 1, second)):
            for h in range(2):
                e = place_of(where_ref, d, h)
                out[slot, h] = lax.dot_general(
                    panel[pl.ds(pl.multiple_of(e * size, size), size)],
                    own_ref[...],
                    (((1,), (1,)), ((), ())),
                    preferred_element_type=f32,
                ).astype(out.dtype)

    out = [jax.ShapeDtypeStruct((2, 2, size, rows), f32), jax.ShapeDtypeStruct((2, 2, size, rows), bf16)]
    return call(
        kernel, out, [SM, VM] + [HBM] * len(arrays),
        [pltpu.VMEM((total, depth), bf16), pltpu.SemaphoreType.DMA((len(copies),))],
        2 * total * rows * depth, 2 * total * (rows + depth), where, own, *arrays,
    )


def sum_pair(keep, got):
    _, _, size, rows = keep.shape

    def kernel(k, g, mine, other):
        other[...] = (k[1] + g[1].astype(f32)).astype(bf16)
        mine[...] = k[0] + g[0].astype(f32)

    out = [jax.ShapeDtypeStruct((2, size, rows), f32), jax.ShapeDtypeStruct((2, size, rows), bf16)]
    return call(kernel, out, [VM] * 2, [], 4 * size * rows, 36 * size * rows, keep, got)


def sum_other(mine, got):
    _, size, rows = mine.shape

    def kernel(m, g, out):
        out[...] = (m[1] + g[1].astype(f32)).astype(bf16)

    return call(kernel, jax.ShapeDtypeStruct((size, rows), bf16), [VM] * 2, [], size * rows, 8 * size * rows, mine, got)


def finish(sums):
    rows = sums[0][2].shape[1]
    t = rows // 3
    flat = [a for three in sums for a in three]

    def kernel(*refs):
        out = refs[-1]
        first = 0
        for i in range(0, len(flat), 3):
            mine, x_part, z_part = refs[i : i + 3]
            size = z_part.shape[0]
            for b in range(size // t):
                part = slice(b * t, (b + 1) * t)
                value = (mine[0, part] + x_part[0, part].astype(f32) + z_part[part].astype(f32)) / N
                out[:, first + b * t : first + (b + 1) * t] = value.T.astype(bf16)
            first += size

    out = jax.ShapeDtypeStruct((rows, 6 * t), bf16)
    return call(kernel, out, [VM] * len(flat), [], 54 * t * t, 60 * t * t * 3, *flat)


def panel_of(arrays, copies, depth):
    cols = arrays[0].shape[1]

    def kernel(*refs):
        refs, out, held, sems, out_sems = refs[:-4], refs[-4], refs[-3], refs[-2], refs[-1]
        started = []
        for i, (ref, src, dst, rows) in enumerate(copies):
            part = held.at[dst // depth, pl.ds(dst % depth, rows)]
            copy = pltpu.make_async_copy(refs[ref].at[pl.ds(src, rows)], part, sems.at[i])
            copy.start()
            started.append(copy)
        leaving = []
        for e in range(8):
            for copy, spec in zip(started, copies):
                if spec[2] // depth == e:
                    copy.wait()
            leaving.append(pltpu.make_async_copy(held.at[e], out.at[e], out_sems.at[e]))
            leaving[-1].start()
        for copy in leaving:
            copy.wait()

    return pl.pallas_call(
        kernel,
        out_shape=jax.ShapeDtypeStruct((8, depth, cols), bf16),
        in_specs=[HBM] * len(arrays),
        out_specs=HBM,
        scratch_shapes=[
            pltpu.VMEM((8, depth, cols), bf16),
            pltpu.SemaphoreType.DMA((len(copies),)),
            pltpu.SemaphoreType.DMA((8,)),
        ],
        cost_estimate=pl.CostEstimate(flops=0, bytes_accessed=32 * depth * cols, transcendentals=0),
        compiler_params=pltpu.CompilerParams(vmem_limit_bytes=VMEM_LIMIT),
    )(*arrays)


def times_x(where, full, panel, total):
    spots = list(full)
    rows, depth = full[spots[0]].shape
    cols = panel.shape[2]
    count = len(spots)
    extra = [] if total is None else [total]

    def kernel(where_ref, *refs):
        parts, panel_ref, refs = refs[:count], refs[count], refs[count + 1 :]
        held, sems = refs[-2:]
        started = []
        for i, spot in enumerate(spots):
            copy = pltpu.make_async_copy(panel_ref.at[place_of(where_ref, *spot)], held.at[i], sems.at[i])
            copy.start()
            started.append(copy)
        y = refs[len(extra)]
        value = None
        for i, copy in enumerate(started):
            copy.wait()
            value = jnp.dot(parts[i][...], held[i], preferred_element_type=f32)
            if i == 0 and extra:
                y[...] = refs[0][...] + value
            elif i == 0:
                y[...] = value
            else:
                y[...] += value
        if extra:
            refs[2][...] = y[...].astype(bf16)

    out = [jax.ShapeDtypeStruct((rows, cols), f32)]
    if extra:
        out.append(jax.ShapeDtypeStruct((rows, cols), bf16))
    return call(
        kernel, out, [SM] + [VM] * count + [HBM] + [VM] * len(extra),
        [pltpu.VMEM((count, depth, cols), bf16), pltpu.SemaphoreType.DMA((count,))],
        2 * count * depth * rows * cols, 2 * count * depth * (rows + cols),
        where, *[full[spot] for spot in spots], panel, *extra,
    )


def arrange(where, full):
    spots = list(full)
    rows, depth = full[spots[0]].shape

    def kernel(where_ref, *refs):
        for spot, part in zip(spots, refs[:8]):
            refs[8][place_of(where_ref, *spot)] = part[...]

    out = jax.ShapeDtypeStruct((8, rows, depth), bf16)
    return call(kernel, out, [SM] + [VM] * 8, [], 0, 32 * rows * depth, where, *[full[spot] for spot in spots])


def times_y(gram, arrays, spots, total, last):
    _, rows, depth = gram.shape
    t = depth // 6
    cols = arrays[0].shape[1]
    copies = []
    for i, a in enumerate(arrays):
        copies.append((i, 0, i * a.shape[0], a.shape[0]))
    extra = ([total] if total is not None else []) + (list(last) if last else [])

    def kernel(gram_ref, *refs):
        ex = refs[: len(extra)]
        ys = refs[len(extra) : len(extra) + len(arrays)]
        out, panel, sems = refs[-3:]
        started = start_copies(copies, ys, panel, sems)
        for copy in started:
            copy.wait()
        for i in range(3):
            part = slice(i * t, (i + 1) * t)
            left = jnp.concatenate([gram_ref[e, part, j * t : (j + 1) * t] for e, j in spots], axis=1)
            value = jnp.dot(left, panel[...], preferred_element_type=f32)
            if total is not None:
                value = ex[0][part] + value
            if last:
                own, y = ex[-2:]
                value = lead_coef * own[part].astype(f32) + square_coef * y[part] + quart_coef * value
            out[part] = value.astype(out.dtype)

    return call(
        kernel, jax.ShapeDtypeStruct((rows, cols), bf16 if last else f32),
        [VM] * (1 + len(extra)) + [HBM] * len(arrays),
        [pltpu.VMEM((len(spots) * t, cols), bf16), pltpu.SemaphoreType.DMA((len(copies),))],
        2 * rows * len(spots) * t * cols, 2 * len(spots) * t * cols, gram, *extra, *arrays,
    )


def spread(mine):
    a1 = swap_x1(mine)
    a3 = swap_x3(mine)
    b0 = swap_zh(mine)
    a1, a3, b0 = together(a1, a3, b0)
    b3 = swap_x3(b0)
    b1 = swap_x1(b0)
    b1, b3 = together(b1, b3)
    a2 = swap_x3(a1)
    b2 = swap_x1(b3)
    early = {(0, 0): mine, (1, 0): a1, (3, 0): a3, (0, 1): b0, (1, 1): b1, (3, 1): b3}
    return early, {(2, 0): a2, (2, 1): b2}


class Reduction:
    def __init__(self, where, own, arrays, copies, size):
        self.keep, self.send = terms_of(where, own, arrays, copies, size)

    def first(self):
        self.got = partner(self.send, True)

    def second(self):
        self.mine, other = sum_pair(self.keep, self.got)
        self.last = partner(other, False)

    def third(self):
        self.z_part = swap_zh(sum_other(self.mine, self.last))

    def result(self):
        return self.mine, self.last, self.z_part


def local(own):
    rows = own.shape[0]
    t = rows // 3
    core = lax.axis_index("c")
    where = jnp.stack([lax.axis_index("x"), lax.axis_index("zh"), 1 + 2 * core, 3 - 2 * core]).astype(jnp.int32)

    queue = [(p, i * t, (plane, slot, i)) for p, (plane, slot) in enumerate(ARRIVAL) for i in range(3)]
    place = {}
    panel_copies = []
    batches = []
    first = 0
    for b, per in enumerate(BATCHES):
        mine = queue[first : first + 8 * per]
        first += 8 * per
        used = sorted({p for p, _, _ in mine})
        copies = []
        for i, (p, row, key) in enumerate(mine):
            e, j = i // per, STARTS[b] + i % per
            place[key] = (e, j)
            panel_copies.append((p, row, (e * 6 + j) * t, t))
            if copies and copies[-1][0] == used.index(p):
                ref, src, dst, count = copies[-1]
                copies[-1] = (ref, src, dst, count + t)
            else:
                copies.append((used.index(p), row, i * t, t))
        batches.append((used, copies, per * t))
    panel_copies.sort(key=lambda c: c[2])

    x = {}

    def reduction(b):
        used, copies, size = batches[b]
        return Reduction(where, own, [x[ARRIVAL[p]] for p in used], copies, size)

    v = own
    r0 = along_y(v)
    w = swap_core(v)
    z = swap_zl(v)
    r0, w = together(r0, w)
    x[0, "v"], x[0, "w"], x[0, "r0"] = v, w, r0
    r1 = along_y(w)
    f = along_y(r0)
    o0 = swap_core(r0)
    one = reduction(0)
    one.first()
    sz = swap_core(z)
    o1 = swap_core(r1)
    r1, f, o0, z, sz, o1, one.got = together(r1, f, o0, z, sz, o1, one.got)
    x[0, "o0"], x[1, "v"], x[0, "r1"], x[1, "w"], x[0, "o1"] = o0, z, r1, sz, o1
    rz0 = along_y(z)
    rz1 = along_y(sz)
    fz = swap_zl(f)
    g = swap_core(f)
    oz0 = swap_core(rz0)
    one.second()
    two = reduction(1)
    two.first()
    rz0, rz1, fz, g, oz0, one.last, two.got = together(rz0, rz1, fz, g, oz0, one.last, two.got)
    x[0, "f"], x[0, "g"], x[1, "r0"], x[1, "o0"], x[1, "r1"], x[1, "f"] = f, g, rz0, oz0, rz1, fz
    oz1 = swap_core(rz1)
    gz = swap_core(fz)
    three = reduction(2)
    one.third()
    two.second()
    oz1, gz, three.send, two.last = together(oz1, gz, three.send, two.last)
    x[1, "o1"], x[1, "g"] = oz1, gz
    three.first()
    two.third()
    four = reduction(3)
    arrays = [x[key] for key in ARRIVAL]
    panel = panel_of(arrays, panel_copies, 6 * t)
    three.got, four.send, two.z_part, one.z_part = together(three.got, four.send, two.z_part, one.z_part)
    four.first()
    three.second()
    three.last, four.got, panel = together(three.last, four.got, panel)
    three.third()
    four.second()
    three.z_part, four.last = together(three.z_part, four.last)
    four.third()
    mine = finish([one.result(), two.result(), three.result(), four.result()])

    same, other = spread(mine)
    part = times_x(where, same, panel, None)[0]
    other[2, 0], other[2, 1], part = together(other[2, 0], other[2, 1], part)
    y, v = times_x(where, other, panel, part)

    def add(total, keys, last=None):
        blocks_of = [place[plane, slot, i] for plane, slot in keys for i in range(3)]
        return times_y(gram, [u[key] for key in keys], blocks_of, total, last)

    u = {}
    r0 = along_y(v)
    w = swap_core(v)
    z = swap_zl(v)
    gram = arrange(where, same | other)
    r0, w, gram = together(r0, w, gram)
    r1 = along_y(w)
    f = along_y(r0)
    o0 = swap_core(r0)
    sz = swap_core(z)
    o1 = swap_core(r1)
    r1, f, o0, z, sz, o1 = together(r1, f, o0, z, sz, o1)
    u[0, "v"], u[0, "w"], u[0, "r0"], u[0, "o0"], u[1, "v"], u[0, "r1"], u[1, "w"], u[0, "o1"] = v, w, r0, o0, z, r1, sz, o1
    rz0 = along_y(z)
    rz1 = along_y(sz)
    fz = swap_zl(f)
    g = swap_core(f)
    oz0 = swap_core(rz0)
    total = add(None, ARRIVAL[:8])
    rz0, rz1, fz, g, oz0, total = together(rz0, rz1, fz, g, oz0, total)
    u[0, "f"], u[0, "g"], u[1, "r0"], u[1, "o0"], u[1, "r1"], u[1, "f"] = f, g, rz0, oz0, rz1, fz
    oz1 = swap_core(rz1)
    gz = swap_core(fz)
    total = add(total, ARRIVAL[8:14])
    u[1, "o1"], u[1, "g"], total = together(oz1, gz, total)
    return add(total, ARRIVAL[14:], [own, y])


def solution(mesh):
    fine = Mesh(mesh.devices.reshape(SIZES), AXES)
    spec = P(ROW, COL)
    return jax.shard_map(local, mesh=fine, in_specs=(spec,), out_specs=spec, check_vma=False)
```

```python
import jax
import jax.numpy as jnp
from jax import lax
from jax.experimental import pallas as pl
from jax.experimental.pallas import tpu as pltpu
from jax.sharding import Mesh, PartitionSpec as P

N = 9216

lead_coef = 3.4445
square_coef = -4.775
quart_coef = 2.0315

AXES = ("zl", "y", "c", "zh", "x")
SIZES = (2, 4, 2, 2, 4)
ROW = ("zl", "y", "c")
COL = ("zh", "x")
f32 = jnp.float32
bf16 = jnp.bfloat16
VMEM_LIMIT = 36 * 2**20

def swap_zl(v):
    return lax.ppermute(v, "zl", [(0, 1), (1, 0)])


def swap_zh(v):
    return lax.ppermute(v, "zh", [(0, 1), (1, 0)])


def swap_core(v):
    return lax.ppermute(v, "c", [(0, 1), (1, 0)])


def swap_x1(v):
    return lax.ppermute(v, "x", [(i, i ^ 1) for i in range(4)])


def swap_x3(v):
    return lax.ppermute(v, "x", [(i, i ^ 3) for i in range(4)])


def partner(v, first):
    pairs = []
    for c in range(2):
        by = 1 if (c == 0) == first else 3
        pairs += [(c * 4 + x, c * 4 + (x ^ by)) for x in range(4)]
    return lax.ppermute(v, ("c", "x"), pairs)


def along_y(v, first=True):
    pairs = []
    for y in range(4):
        for c in range(2):
            by = 1 if (c == 0) == first else -1
            pairs.append((y * 2 + c, (y + by) % 4 * 2 + c))
    return lax.ppermute(v, ("y", "c"), pairs)


def together(*values):
    return lax.optimization_barrier(values)


ARRIVAL = ((0, "v"), (0, "r0"), (1, "v"), (0, "r1"), (0, "f"), (1, "r0"), (1, "r1"), (1, "f"))
BATCHES = 3


VM = pl.BlockSpec(memory_space=pltpu.VMEM)
SM = pl.BlockSpec(memory_space=pltpu.SMEM)
HBM = pl.BlockSpec(memory_space=pltpu.HBM)


def call(kernel, out_shape, in_specs, scratch, *args):
    outs = jax.tree.map(lambda _: VM, out_shape)
    return pl.pallas_call(
        kernel,
        out_shape=out_shape,
        in_specs=in_specs,
        out_specs=outs,
        scratch_shapes=scratch,
        cost_estimate=pl.CostEstimate(flops=0, bytes_accessed=0, transcendentals=0),
        compiler_params=pltpu.CompilerParams(vmem_limit_bytes=VMEM_LIMIT),
    )(*args)


def place_of(where_ref, d, h):
    return jnp.bitwise_xor(where_ref[0], d) * 2 + jnp.bitwise_xor(where_ref[1], h)


def start_copies(copies, refs, panel, sems):
    started = []
    for i, (ref, src, dst, rows) in enumerate(copies):
        copy = pltpu.make_async_copy(refs[ref].at[pl.ds(src, rows)], panel.at[pl.ds(dst, rows)], sems.at[i])
        copy.start()
        started.append(copy)
    return started


def terms_of(where, own, sibling, arrays, copies, send):
    rows, depth = own.shape
    t = rows // 3

    def kernel(where_ref, own_ref, sib_ref, *refs):
        refs, out, panel, sems = refs[:-3], refs[-3], refs[-2], refs[-1]
        for copy in start_copies(copies, refs, panel, sems):
            copy.wait()
        for slot, d in enumerate((where_ref[2], 2) if send else (0, where_ref[3])):
            x = jnp.bitwise_xor(where_ref[0], d)
            pair = panel[pl.ds(pl.multiple_of(x * 2 * t, 2 * t), 2 * t)]
            for i, left in enumerate((own_ref, sib_ref)):
                value = lax.dot_general(
                    left[...], pair, (((1,), (1,)), ((), ())), preferred_element_type=f32
                ).astype(out.dtype)
                for z in range(2):
                    h = jnp.bitwise_xor(where_ref[1], z)
                    out[slot, h, i * rows : (i + 1) * rows] = value[:, z * t : (z + 1) * t]

    return call(
        kernel, jax.ShapeDtypeStruct((2, 2, 2 * rows, t), bf16 if send else f32),
        [SM, VM, VM] + [HBM] * len(arrays),
        [pltpu.VMEM((8 * t, depth), bf16), pltpu.SemaphoreType.DMA((len(copies),))],
        where, own, sibling, *arrays,
    )


def sum_pair(keep, got):
    shape = keep.shape[1:]

    def kernel(k, g, mine, other):
        other[...] = (k[1] + g[1].astype(f32)).astype(bf16)
        mine[...] = k[0] + g[0].astype(f32)

    return call(kernel, [jax.ShapeDtypeStruct(shape, f32), jax.ShapeDtypeStruct(shape, bf16)], [VM] * 2, [], keep, got)


def sum_other(mine, got):
    def kernel(m, g, out):
        out[...] = (m[1] + g[1].astype(f32)).astype(bf16)

    return call(kernel, jax.ShapeDtypeStruct(mine.shape[1:], bf16), [VM] * 2, [], mine, got)


def finish(sums):
    rows, t = sums[0][2].shape
    flat = [a for three in sums for a in three]

    def kernel(*refs):
        out = refs[-1]
        for b in range(len(sums)):
            mine, x_part, z_part = refs[3 * b : 3 * b + 3]
            value = (mine[0] + x_part[0].astype(f32) + z_part[...].astype(f32)) / N
            out[:, b * t : (b + 1) * t] = value.astype(bf16)

    return call(kernel, jax.ShapeDtypeStruct((rows, len(sums) * t), bf16), [VM] * len(flat), [], *flat)


def times_x(where, full, arrays, copies, total, half, dtype):
    spots = list(full)
    both, depth = full[spots[0]].shape
    cols = arrays[0].shape[1]
    count = len(spots)
    extra = [] if total is None else [total]
    part = slice(0, both) if half is None else slice(half * both // 2, (half + 1) * both // 2)
    rows = part.stop - part.start
    lists = [[spec for spec in copies if spec[2] // depth == e] for e in range(8)]

    def kernel(where_ref, *refs):
        slices, pieces, refs = refs[:count], refs[count : count + len(arrays)], refs[count + len(arrays) :]
        out, held, sems = refs[-3:]

        def copy_of(i, j, spec):
            ref, src, dst, size = spec
            target = held.at[pl.ds(i * depth + dst % depth, size)]
            return pltpu.make_async_copy(pieces[ref].at[pl.ds(src, size)], target, sems.at[i, j])

        for i, spot in enumerate(spots):
            place = place_of(where_ref, *spot)
            for e in range(8):
                @pl.when(place == e)
                def _(i=i, e=e):
                    for j, spec in enumerate(lists[e]):
                        copy_of(i, j, spec).start()

        for i in range(0, count, 2):
            for k in (i, i + 1):
                for j, spec in enumerate(lists[0]):
                    copy_of(k, j, spec).wait()
            left = jnp.concatenate([slices[i][part], slices[i + 1][part]], axis=1)
            value = jnp.dot(left, held[i * depth : (i + 2) * depth], preferred_element_type=f32)
            if i > 0:
                value = out[...] + value
            elif extra:
                value = refs[0][part] + value
            out[...] = value.astype(dtype)

    return call(
        kernel, jax.ShapeDtypeStruct((rows, cols), dtype), [SM] + [VM] * count + [HBM] * len(arrays) + [VM] * len(extra),
        [pltpu.VMEM((count * depth, cols), bf16), pltpu.SemaphoreType.DMA((count, len(lists[0])))],
        where, *[full[spot] for spot in spots], *arrays, *extra,
    )


def add_rounded(mine, got):
    def kernel(m, g, y, v):
        value = m[...] + g[...].astype(f32)
        y[...] = value
        v[...] = value.astype(bf16)

    out = [jax.ShapeDtypeStruct(mine.shape, f32), jax.ShapeDtypeStruct(mine.shape, bf16)]
    return call(kernel, out, [VM] * 2, [], mine, got)


def arrange(where, full):
    spots = list(full)

    def kernel(where_ref, *refs):
        for spot, part in zip(spots, refs[:8]):
            refs[8][place_of(where_ref, *spot)] = part[...]

    out = jax.ShapeDtypeStruct((8,) + full[spots[0]].shape, bf16)
    return call(kernel, out, [SM] + [VM] * 8, [], where, *[full[spot] for spot in spots])


def times_y(gram, arrays, spots, total, half, dtype):
    _, both, depth = gram.shape
    t = depth // BATCHES
    cols = arrays[0].shape[1]
    copies = [(i, 0, i * a.shape[0], a.shape[0]) for i, a in enumerate(arrays)]
    extra = [] if total is None else [total]
    halves = (0, 1) if half is None else (half,)
    rows = both // 2

    def kernel(gram_ref, *refs):
        ys = refs[len(extra) : len(extra) + len(arrays)]
        out, panel, sems = refs[-3:]
        for copy in start_copies(copies, ys, panel, sems):
            copy.wait()
        for i, one in enumerate(halves):
            part = slice(one * rows, (one + 1) * rows)
            left = jnp.concatenate([gram_ref[e, part, j * t : (j + 1) * t] for e, j in spots], axis=1)
            value = jnp.dot(left, panel[...], preferred_element_type=f32)
            if extra:
                value = refs[0][part] + value
            out[i * rows : (i + 1) * rows] = value.astype(dtype)

    return call(
        kernel, jax.ShapeDtypeStruct((rows * len(halves), cols), dtype), [VM] * (1 + len(extra)) + [HBM] * len(arrays),
        [pltpu.VMEM((len(spots) * t, cols), bf16), pltpu.SemaphoreType.DMA((len(copies),))],
        gram, *extra, *arrays,
    )


def result(own, y, mine, got):
    def kernel(own_ref, y_ref, m, g, out):
        square = m[...] + g[...].astype(f32)
        out[...] = (lead_coef * own_ref[...].astype(f32) + square_coef * y_ref[...] + quart_coef * square).astype(bf16)

    return call(kernel, jax.ShapeDtypeStruct(own.shape, bf16), [VM] * 4, [], own, y, mine, got)


def local(own):
    rows = own.shape[0]
    t = rows // 3
    core = lax.axis_index("c")
    where = jnp.stack([lax.axis_index("x"), lax.axis_index("zh"), 1 + 2 * core, 3 - 2 * core]).astype(jnp.int32)

    place = {}
    panel_copies = []
    batches = []
    queue = [(p, i, (plane, slot, i)) for p, (plane, slot) in enumerate(ARRIVAL) for i in range(3)]
    for b in range(BATCHES):
        mine = queue[8 * b : 8 * b + 8]
        used = sorted({p for p, _, _ in mine})
        copies = []
        for e, (p, i, key) in enumerate(mine):
            place[key] = (e, b)
            panel_copies.append((p, i * t, (e * BATCHES + b) * t, t))
            copies.append((used.index(p), i * t, e * t, t))
        batches.append((used, copies))
    panel_copies.sort(key=lambda c: c[2])
    x = {}

    def terms(b, send):
        used, copies = batches[b]
        return terms_of(where, own, w, [x[ARRIVAL[p]] for p in used], copies, send)

    r0 = along_y(own)
    w = swap_core(own)
    z = swap_zl(own)
    r1 = along_y(own, False)
    r0, w, z, r1 = together(r0, w, z, r1)
    x[0, "v"], x[0, "r0"], x[1, "v"], x[0, "r1"] = own, r0, z, r1
    rz0 = along_y(z)
    f = along_y(r0)
    rz1 = swap_zl(r1)
    got1 = partner(terms(0, True), True)
    keep1 = terms(0, False)
    rz0, f, rz1, got1, keep1 = together(rz0, f, rz1, got1, keep1)
    x[0, "f"], x[1, "r0"], x[1, "r1"] = f, rz0, rz1
    fz = along_y(rz0)
    mine1, other1 = sum_pair(keep1, got1)
    last1 = partner(other1, False)
    send2 = terms(1, True)
    got2 = partner(send2, True)
    keep2 = terms(1, False)
    fz, keep2 = together(fz, keep2)
    x[1, "f"] = fz
    send3 = terms(2, True)
    got2, send3, last1 = together(got2, send3, last1)
    got3 = partner(send3, True)
    keep3 = terms(2, False)
    z1 = swap_zh(sum_other(mine1, last1))
    mine2, other2 = sum_pair(keep2, got2)
    last2 = partner(other2, False)
    got3, keep3, last2, z1 = together(got3, keep3, last2, z1)
    z2 = swap_zh(sum_other(mine2, last2))
    mine3, other3 = sum_pair(keep3, got3)
    last3 = partner(other3, False)
    last3, z2 = together(last3, z2)
    z3 = swap_zh(sum_other(mine3, last3))
    mine = finish([(mine1, last1, z1), (mine2, last2, z2), (mine3, last3, z3)])
    arrays = [x[key] for key in ARRIVAL]

    a1 = swap_x1(mine)
    a3 = swap_x3(mine)
    b0 = swap_zh(mine)
    a1, a3, b0 = together(a1, a3, b0)
    b3 = swap_x3(b0)
    b1 = swap_x1(b0)
    a2 = swap_x3(a1)
    near = {(0, 0): mine, (1, 0): a1, (3, 0): a3, (0, 1): b0}
    part = times_x(where, near, arrays, panel_copies, None, None, f32)
    b1, b3, part = together(b1, b3, part)
    b2 = swap_x1(b3)
    next_ones = {(1, 1): b1, (3, 1): b3}
    part = times_x(where, next_ones, arrays, panel_copies, part, None, f32)
    a2, b2, part = together(a2, b2, part)
    late = {(2, 0): a2, (2, 1): b2}
    give = times_x(where, late, arrays, panel_copies, part, 1, bf16)
    got = swap_core(give)
    y = times_x(where, late, arrays, panel_copies, part, 0, f32)
    got, y = together(got, y)
    y, v = add_rounded(y, got)

    def add(total, keys, half=None, dtype=f32):
        spots = [place[plane, slot, i] for plane, slot in keys for i in range(3)]
        return times_y(gram, [u[key] for key in keys], spots, total, half, dtype)

    u = {}
    r0 = along_y(v)
    r1 = along_y(v, False)
    z = swap_zl(v)
    gram = arrange(where, near | next_ones | late)
    r0, z, r1, gram = together(r0, z, r1, gram)
    u[0, "v"], u[0, "r0"], u[1, "v"], u[0, "r1"] = v, r0, z, r1
    rz0 = along_y(z)
    f = along_y(r0)
    rz1 = swap_zl(r1)
    total = add(None, ARRIVAL[:4])
    rz0, f, rz1, total = together(rz0, f, rz1, total)
    u[0, "f"], u[1, "r0"], u[1, "r1"] = f, rz0, rz1
    fz = along_y(rz0)
    total = add(total, ARRIVAL[4:7])
    fz, total = together(fz, total)
    u[1, "f"] = fz
    got = swap_core(add(total, ARRIVAL[7:], 1, bf16))
    mine = add(total, ARRIVAL[7:], 0)
    got, mine = together(got, mine)
    return result(own, y, mine, got)


def solution(mesh):
    fine = Mesh(mesh.devices.reshape(SIZES), AXES)
    spec = P(ROW, COL)
    return jax.shard_map(local, mesh=fine, in_specs=(spec,), out_specs=spec, check_vma=False)
```

```python
import jax
import jax.numpy as jnp
from jax import lax
from jax.experimental import pallas as pl
from jax.experimental.pallas import tpu as pltpu
from jax.sharding import Mesh, PartitionSpec as P

N = 9216

lead_coef = 3.4445
square_coef = -4.775
quart_coef = 2.0315

AXES = ("zl", "y", "c", "zh", "x")
SIZES = (2, 4, 2, 2, 4)
ROW = ("zl", "y", "c")
COL = ("zh", "x")
f32 = jnp.float32
bf16 = jnp.bfloat16
VMEM_LIMIT = 36 * 2**20

def swap_zl(v):
    return lax.ppermute(v, "zl", [(0, 1), (1, 0)])


def swap_zh(v):
    return lax.ppermute(v, "zh", [(0, 1), (1, 0)])


def swap_core(v):
    return lax.ppermute(v, "c", [(0, 1), (1, 0)])


def swap_x1(v):
    return lax.ppermute(v, "x", [(i, i ^ 1) for i in range(4)])


def swap_x3(v):
    return lax.ppermute(v, "x", [(i, i ^ 3) for i in range(4)])


def partner(v, first):
    pairs = []
    for c in range(2):
        by = 1 if (c == 0) == first else 3
        pairs += [(c * 4 + x, c * 4 + (x ^ by)) for x in range(4)]
    return lax.ppermute(v, ("c", "x"), pairs)


def along_y(v, first=True):
    pairs = []
    for y in range(4):
        for c in range(2):
            by = 1 if (c == 0) == first else -1
            pairs.append((y * 2 + c, (y + by) % 4 * 2 + c))
    return lax.ppermute(v, ("y", "c"), pairs)


def together(*values):
    return lax.optimization_barrier(values)


EARLY = ((0, "v"), (0, "r0"), (1, "v"), (0, "r1"))
MIDDLE = ((0, "f"), (1, "r0"), (1, "r1"))
LATE = ((1, "f"),)
ARRIVAL = EARLY + MIDDLE + LATE


VM = pl.BlockSpec(memory_space=pltpu.VMEM)
SM = pl.BlockSpec(memory_space=pltpu.SMEM)
HBM = pl.BlockSpec(memory_space=pltpu.HBM)


def call(kernel, out_shape, in_specs, scratch, *args):
    outs = jax.tree.map(lambda _: VM, out_shape)
    return pl.pallas_call(
        kernel,
        out_shape=out_shape,
        in_specs=in_specs,
        out_specs=outs,
        scratch_shapes=scratch,
        cost_estimate=pl.CostEstimate(flops=0, bytes_accessed=0, transcendentals=0),
        compiler_params=pltpu.CompilerParams(vmem_limit_bytes=VMEM_LIMIT),
    )(*args)


def place_of(where_ref, d, h):
    return jnp.bitwise_xor(where_ref[0], d) * 2 + jnp.bitwise_xor(where_ref[1], h)


def start_copies(copies, refs, panel, sems):
    started = []
    for i, (ref, src, dst, rows) in enumerate(copies):
        copy = pltpu.make_async_copy(refs[ref].at[pl.ds(src, rows)], panel.at[pl.ds(dst, rows)], sems.at[i])
        copy.start()
        started.append(copy)
    return started


def terms_of(where, own, sibling, arrays, send):
    rows, depth = own.shape
    eighth = rows // 8
    count = len(arrays)
    copies = [(i, 0, i * rows, rows) for i in range(count)]

    def kernel(where_ref, own_ref, sib_ref, *refs):
        refs, out, panel, sems = refs[:-3], refs[-3], refs[-2], refs[-1]
        for copy in start_copies(copies, refs, panel, sems):
            copy.wait()
        parts = []
        for d in (where_ref[2], 2) if send else (0, where_ref[3]):
            x = jnp.bitwise_xor(where_ref[0], d)
            for p in range(count):
                first = pl.multiple_of(p * rows + x * 2 * eighth, 2 * eighth)
                parts.append(panel[pl.ds(first, 2 * eighth)])
        left = jnp.concatenate(parts, axis=0)
        for i, right in enumerate((own_ref, sib_ref)):
            value = lax.dot_general(
                left, right[...], (((1,), (1,)), ((), ())), preferred_element_type=f32
            ).astype(out.dtype)
            for slot in range(2):
                for p in range(count):
                    for z in range(2):
                        first = ((slot * count + p) * 2 + z) * eighth
                        h = jnp.bitwise_xor(where_ref[1], z)
                        target = (slot, h, slice(p * eighth, (p + 1) * eighth), slice(i * rows, (i + 1) * rows))
                        out[target] = value[first : first + eighth]

    return call(
        kernel, jax.ShapeDtypeStruct((2, 2, count * eighth, 2 * rows), bf16 if send else f32),
        [SM, VM, VM] + [HBM] * count,
        [pltpu.VMEM((count * rows, depth), bf16), pltpu.SemaphoreType.DMA((count,))],
        where, own, sibling, *arrays,
    )


def sum_pair(*pairs):
    sizes = [keep.shape[2] for keep, _ in pairs]
    flat = [a for pair in pairs for a in pair]

    def kernel(*refs):
        mine, other = refs[-2:]
        first = 0
        for b, size in enumerate(sizes):
            k, g = refs[2 * b : 2 * b + 2]
            other[:, first : first + size] = (k[1] + g[1].astype(f32)).astype(bf16)
            mine[:, first : first + size] = k[0] + g[0].astype(f32)
            first += size

    shape = (2, sum(sizes), pairs[0][0].shape[3])
    out = [jax.ShapeDtypeStruct(shape, f32), jax.ShapeDtypeStruct(shape, bf16)]
    return call(kernel, out, [VM] * len(flat), [], *flat)


def sum_other(*pairs):
    sizes = [mine.shape[1] for mine, _ in pairs]
    flat = [a for pair in pairs for a in pair]

    def kernel(*refs):
        first = 0
        for b, size in enumerate(sizes):
            refs[-1][first : first + size] = (refs[2 * b][1] + refs[2 * b + 1][1].astype(f32)).astype(bf16)
            first += size

    out = jax.ShapeDtypeStruct((sum(sizes), pairs[0][0].shape[2]), bf16)
    return call(kernel, out, [VM] * len(flat), [], *flat)


def finish(pairs, z_parts):
    sizes = [mine.shape[1] for mine, _ in pairs]
    rows = pairs[0][0].shape[2]
    flat = [a for pair in pairs for a in pair] + z_parts

    def kernel(*refs):
        values = []
        for b in range(len(sizes)):
            values.append(refs[2 * b][0] + refs[2 * b + 1][0].astype(f32))
        value = jnp.concatenate(values, axis=0)
        z_part = jnp.concatenate([ref[...] for ref in refs[2 * len(sizes) : -1]], axis=0)
        refs[-1][...] = ((value + z_part.astype(f32)) / N).T.astype(bf16)

    return call(kernel, jax.ShapeDtypeStruct((rows, sum(sizes)), bf16), [VM] * len(flat), [], *flat)


def stack_blocks(arrays):
    shape = (len(arrays),) + arrays[0].shape

    def kernel(*refs):
        refs, out, held, sems, out_sems = refs[:-4], refs[-4], refs[-3], refs[-2], refs[-1]
        started, leaving = [], []
        for i, ref in enumerate(refs):
            started.append(pltpu.make_async_copy(ref, held.at[i], sems.at[i]))
            started[-1].start()
        for i, copy in enumerate(started):
            copy.wait()
            leaving.append(pltpu.make_async_copy(held.at[i], out.at[i], out_sems.at[i]))
            leaving[-1].start()
        for copy in leaving:
            copy.wait()

    return pl.pallas_call(
        kernel,
        out_shape=jax.ShapeDtypeStruct(shape, bf16),
        in_specs=[HBM] * len(arrays),
        out_specs=HBM,
        scratch_shapes=[
            pltpu.VMEM(shape, bf16),
            pltpu.SemaphoreType.DMA((len(arrays),)),
            pltpu.SemaphoreType.DMA((len(arrays),)),
        ],
        cost_estimate=pl.CostEstimate(flops=0, bytes_accessed=0, transcendentals=0),
        compiler_params=pltpu.CompilerParams(vmem_limit_bytes=VMEM_LIMIT),
    )(*arrays)


def times_x(where, full, panel, total, half, dtype):
    spots = list(full)
    both, depth = full[spots[0]].shape
    blocks, block, cols = panel.shape
    eighth = block // 8
    count = len(spots)
    extra = [] if total is None else [total]
    part = slice(0, both) if half is None else slice(half * both // 2, (half + 1) * both // 2)
    rows = part.stop - part.start

    def kernel(where_ref, *refs):
        slices, panel_ref, refs = refs[:count], refs[count], refs[count + 1 :]
        out, held, sems = refs[-3:]
        started = []
        for i, spot in enumerate(spots):
            first = pl.multiple_of(place_of(where_ref, *spot) * eighth, eighth)
            copy = pltpu.make_async_copy(panel_ref.at[:, pl.ds(first, eighth)], held.at[i], sems.at[i])
            copy.start()
            started.append(copy)
        for i in range(0, count, 2):
            group = range(i, min(i + 2, count))
            for k in group:
                started[k].wait()
            left = jnp.concatenate([slices[k][part] for k in group], axis=1)
            right = held[i : i + len(group)].reshape(len(group) * depth, cols)
            value = jnp.dot(left, right, preferred_element_type=f32)
            if i > 0:
                value = out[...] + value
            elif extra:
                value = refs[0][part] + value
            out[...] = value.astype(dtype)

    return call(
        kernel, jax.ShapeDtypeStruct((rows, cols), dtype), [SM] + [VM] * count + [HBM] + [VM] * len(extra),
        [pltpu.VMEM((count, blocks, eighth, cols), bf16), pltpu.SemaphoreType.DMA((count,))],
        where, *[full[spot] for spot in spots], panel, *extra,
    )


def add_rounded(mine, got):
    def kernel(m, g, y, v):
        value = m[...] + g[...].astype(f32)
        y[...] = value
        v[...] = value.astype(bf16)

    out = [jax.ShapeDtypeStruct(mine.shape, f32), jax.ShapeDtypeStruct(mine.shape, bf16)]
    return call(kernel, out, [VM] * 2, [], mine, got)


def arrange(where, full):
    spots = list(full)
    both, depth = full[spots[0]].shape
    eighth = depth // 8

    def kernel(where_ref, *refs):
        out, held = refs[8:]
        for spot, part in zip(spots, refs[:8]):
            held[place_of(where_ref, *spot)] = part[...]
        for p in range(8):
            out[p] = jnp.concatenate([held[e, :, p * eighth : (p + 1) * eighth] for e in range(8)], axis=1)

    out = jax.ShapeDtypeStruct((8, both, depth), bf16)
    return call(
        kernel, out, [SM] + [VM] * 8, [pltpu.VMEM((8, both, depth), bf16)], where, *[full[spot] for spot in spots]
    )


def times_y(gram, arrays, first, total, half, dtype):
    _, both, depth = gram.shape
    cols = arrays[0].shape[1]
    copies = [(i, 0, i * depth, depth) for i in range(len(arrays))]
    extra = [] if total is None else [total]
    halves = (0, 1) if half is None else (half,)
    rows = both // 2

    def kernel(gram_ref, *refs):
        ys = refs[len(extra) : len(extra) + len(arrays)]
        out, panel, sems = refs[-3:]
        for copy in start_copies(copies, ys, panel, sems):
            copy.wait()
        for i, one in enumerate(halves):
            part = slice(one * rows, (one + 1) * rows)
            left = jnp.concatenate([gram_ref[first + p, part] for p in range(len(arrays))], axis=1)
            value = jnp.dot(left, panel[...], preferred_element_type=f32)
            if extra:
                value = refs[0][part] + value
            out[i * rows : (i + 1) * rows] = value.astype(dtype)

    return call(
        kernel, jax.ShapeDtypeStruct((rows * len(halves), cols), dtype), [VM] * (1 + len(extra)) + [HBM] * len(arrays),
        [pltpu.VMEM((len(arrays) * depth, cols), bf16), pltpu.SemaphoreType.DMA((len(arrays),))],
        gram, *extra, *arrays,
    )


def result(own, y, mine, got):
    def kernel(own_ref, y_ref, m, g, out):
        square = m[...] + g[...].astype(f32)
        out[...] = (lead_coef * own_ref[...].astype(f32) + square_coef * y_ref[...] + quart_coef * square).astype(bf16)

    return call(kernel, jax.ShapeDtypeStruct(own.shape, bf16), [VM] * 4, [], own, y, mine, got)


def local(own):
    core = lax.axis_index("c")
    where = jnp.stack([lax.axis_index("x"), lax.axis_index("zh"), 1 + 2 * core, 3 - 2 * core]).astype(jnp.int32)
    x = {}

    def terms(keys, send):
        return terms_of(where, own, w, [x[key] for key in keys], send)

    z = swap_zl(own)
    r0 = along_y(own)
    r1 = along_y(own, False)
    w = swap_core(own)
    r0, w, z, r1 = together(r0, w, z, r1)
    x[0, "v"], x[0, "r0"], x[1, "v"], x[0, "r1"] = own, r0, z, r1
    rz1 = swap_zl(r1)
    rz0 = along_y(z)
    f = along_y(r1, False)
    got1 = partner(terms(EARLY, True), True)
    keep1 = terms(EARLY, False)
    rz0, f, rz1, keep1 = together(rz0, f, rz1, keep1)
    x[0, "f"], x[1, "r0"], x[1, "r1"] = f, rz0, rz1
    fz = along_y(rz0)
    send2 = terms(MIDDLE, True)
    got2 = partner(send2, True)
    keep2 = terms(MIDDLE, False)
    fz, keep2, got1 = together(fz, keep2, got1)
    x[1, "f"] = fz
    got3 = partner(terms(LATE, True), True)
    mine1, other1 = sum_pair((keep1, got1))
    last1 = partner(other1, False)
    keep3 = terms(LATE, False)
    got2, keep3, got3, last1 = together(got2, keep3, got3, last1)
    mine2, other2 = sum_pair((keep2, got2), (keep3, got3))
    z1 = swap_zh(sum_other((mine1, last1)))
    last2 = partner(other2, False)
    last2, z1 = together(last2, z1)
    z2 = swap_zh(sum_other((mine2, last2)))
    mine = finish([(mine1, last1), (mine2, last2)], [z1, z2])
    b0 = swap_zh(mine)
    a1 = swap_x1(mine)
    a3 = swap_x3(mine)
    panel = stack_blocks([x[key] for key in ARRIVAL])
    a1, a3, b0, panel = together(a1, a3, b0, panel)
    b3 = swap_x3(b0)
    b1 = swap_x1(b0)
    a2 = swap_x3(a1)
    near = {(0, 0): mine, (1, 0): a1, (3, 0): a3, (0, 1): b0}
    part = times_x(where, near, panel, None, None, f32)
    b1, b3, part = together(b1, b3, part)
    b2 = swap_x1(b3)
    next_ones = {(1, 1): b1, (3, 1): b3}
    part = times_x(where, next_ones, panel, part, None, f32)
    a2, b2, part = together(a2, b2, part)
    late = {(2, 0): a2, (2, 1): b2}
    give = times_x(where, late, panel, part, 1, bf16)
    got = swap_core(give)
    y = times_x(where, late, panel, part, 0, f32)
    got, y = together(got, y)
    y, v = add_rounded(y, got)

    def add(total, keys, half=None, dtype=f32):
        return times_y(gram, [u[key] for key in keys], ARRIVAL.index(keys[0]), total, half, dtype)

    u = {}
    z = swap_zl(v)
    r0 = along_y(v)
    r1 = along_y(v, False)
    gram = arrange(where, near | next_ones | late)
    r0, z, r1, gram = together(r0, z, r1, gram)
    u[0, "v"], u[0, "r0"], u[1, "v"], u[0, "r1"] = v, r0, z, r1
    rz1 = swap_zl(r1)
    rz0 = along_y(z)
    f = along_y(r1, False)
    total = add(None, EARLY)
    rz0, f, rz1, total = together(rz0, f, rz1, total)
    u[0, "f"], u[1, "r0"], u[1, "r1"] = f, rz0, rz1
    fz = along_y(rz0)
    total = add(total, MIDDLE)
    fz, total = together(fz, total)
    u[1, "f"] = fz
    got = swap_core(add(total, LATE, 1, bf16))
    mine = add(total, LATE, 0)
    got, mine = together(got, mine)
    return result(own, y, mine, got)


def solution(mesh):
    fine = Mesh(mesh.devices.reshape(SIZES), AXES)
    spec = P(ROW, COL)
    return jax.shard_map(local, mesh=fine, in_specs=(spec,), out_specs=spec, check_vma=False)
```

```python
import jax
import jax.numpy as jnp
from jax import lax
from jax.experimental import pallas as pl
from jax.experimental.pallas import tpu as pltpu
from jax.sharding import Mesh, PartitionSpec as P

N = 9216

lead_coef = 3.4445
square_coef = -4.775
quart_coef = 2.0315

AXES = ("zl", "y", "c", "zh", "x")
SIZES = (2, 4, 2, 2, 4)
ROW = ("zl", "y", "c")
COL = ("zh", "x")
f32 = jnp.float32
bf16 = jnp.bfloat16
VMEM_LIMIT = 36 * 2**20

def swap_zl(v):
    return lax.ppermute(v, "zl", [(0, 1), (1, 0)])


def swap_zh(v):
    return lax.ppermute(v, "zh", [(0, 1), (1, 0)])


def swap_core(v):
    return lax.ppermute(v, "c", [(0, 1), (1, 0)])


def swap_x1(v):
    return lax.ppermute(v, "x", [(i, i ^ 1) for i in range(4)])


def swap_x3(v):
    return lax.ppermute(v, "x", [(i, i ^ 3) for i in range(4)])


def partner(v, first):
    pairs = []
    for c in range(2):
        by = 1 if (c == 0) == first else 3
        pairs += [(c * 4 + x, c * 4 + (x ^ by)) for x in range(4)]
    return lax.ppermute(v, ("c", "x"), pairs)


def along_y(v, first=True):
    pairs = []
    for y in range(4):
        for c in range(2):
            by = 1 if (c == 0) == first else -1
            pairs.append((y * 2 + c, (y + by) % 4 * 2 + c))
    return lax.ppermute(v, ("y", "c"), pairs)


def together(*values):
    return lax.optimization_barrier(values)


OWN = ((0, "v"),)
EARLY = ((0, "r0"), (1, "v"), (0, "r1"))
MIDDLE = ((0, "f"), (1, "r0"), (1, "r1"))
LATE = ((1, "f"),)
ARRIVAL = OWN + EARLY + MIDDLE + LATE


VM = pl.BlockSpec(memory_space=pltpu.VMEM)
SM = pl.BlockSpec(memory_space=pltpu.SMEM)
HBM = pl.BlockSpec(memory_space=pltpu.HBM)


def call(kernel, out_shape, in_specs, scratch, *args):
    outs = jax.tree.map(lambda _: VM, out_shape)
    return pl.pallas_call(
        kernel,
        out_shape=out_shape,
        in_specs=in_specs,
        out_specs=outs,
        scratch_shapes=scratch,
        cost_estimate=pl.CostEstimate(flops=0, bytes_accessed=0, transcendentals=0),
        compiler_params=pltpu.CompilerParams(vmem_limit_bytes=VMEM_LIMIT),
    )(*args)


def place_of(where_ref, d, h):
    return jnp.bitwise_xor(where_ref[0], d) * 2 + jnp.bitwise_xor(where_ref[1], h)


def start_copies(copies, refs, panel, sems):
    started = []
    for i, (ref, src, dst, rows) in enumerate(copies):
        copy = pltpu.make_async_copy(refs[ref].at[pl.ds(src, rows)], panel.at[pl.ds(dst, rows)], sems.at[i])
        copy.start()
        started.append(copy)
    return started


def terms_of(where, own, sibling, arrays, send):
    rows, depth = own.shape
    eighth = rows // 8
    count = len(arrays)
    copies = [(i, 0, i * rows, rows) for i in range(count)]

    def kernel(where_ref, own_ref, sib_ref, *refs):
        refs, out, panel, sems = refs[:-3], refs[-3], refs[-2], refs[-1]
        for copy in start_copies(copies, refs, panel, sems):
            copy.wait()
        parts = []
        for d in (where_ref[2], 2) if send else (0, where_ref[3]):
            x = jnp.bitwise_xor(where_ref[0], d)
            for p in range(count):
                first = pl.multiple_of(p * rows + x * 2 * eighth, 2 * eighth)
                parts.append(panel[pl.ds(first, 2 * eighth)])
        left = jnp.concatenate(parts, axis=0)
        for i, right in enumerate((own_ref, sib_ref)):
            value = lax.dot_general(
                left, right[...], (((1,), (1,)), ((), ())), preferred_element_type=f32
            ).astype(out.dtype)
            for slot in range(2):
                for p in range(count):
                    for z in range(2):
                        first = ((slot * count + p) * 2 + z) * eighth
                        h = jnp.bitwise_xor(where_ref[1], z)
                        target = (slot, h, slice(p * eighth, (p + 1) * eighth), slice(i * rows, (i + 1) * rows))
                        out[target] = value[first : first + eighth]

    return call(
        kernel, jax.ShapeDtypeStruct((2, 2, count * eighth, 2 * rows), bf16 if send else f32),
        [SM, VM, VM] + [HBM] * count,
        [pltpu.VMEM((count * rows, depth), bf16), pltpu.SemaphoreType.DMA((count,))],
        where, own, sibling, *arrays,
    )


def sum_pair(*pairs):
    sizes = [keep.shape[2] for keep, _ in pairs]
    flat = [a for pair in pairs for a in pair]

    def kernel(*refs):
        mine, other = refs[-2:]
        first = 0
        for b, size in enumerate(sizes):
            k, g = refs[2 * b : 2 * b + 2]
            other[:, first : first + size] = (k[1] + g[1].astype(f32)).astype(bf16)
            mine[:, first : first + size] = k[0] + g[0].astype(f32)
            first += size

    shape = (2, sum(sizes), pairs[0][0].shape[3])
    out = [jax.ShapeDtypeStruct(shape, f32), jax.ShapeDtypeStruct(shape, bf16)]
    return call(kernel, out, [VM] * len(flat), [], *flat)


def sum_other(*pairs):
    sizes = [mine.shape[1] for mine, _ in pairs]
    flat = [a for pair in pairs for a in pair]

    def kernel(*refs):
        first = 0
        for b, size in enumerate(sizes):
            refs[-1][first : first + size] = (refs[2 * b][1] + refs[2 * b + 1][1].astype(f32)).astype(bf16)
            first += size

    out = jax.ShapeDtypeStruct((sum(sizes), pairs[0][0].shape[2]), bf16)
    return call(kernel, out, [VM] * len(flat), [], *flat)


def finish(pairs, z_parts):
    sizes = [mine.shape[1] for mine, _ in pairs]
    rows = pairs[0][0].shape[2]
    flat = [a for pair in pairs for a in pair] + z_parts

    def kernel(*refs):
        values = []
        for b in range(len(sizes)):
            values.append(refs[2 * b][0] + refs[2 * b + 1][0].astype(f32))
        value = jnp.concatenate(values, axis=0)
        z_part = jnp.concatenate([ref[...] for ref in refs[2 * len(sizes) : -1]], axis=0)
        refs[-1][...] = ((value + z_part.astype(f32)) / N).T.astype(bf16)

    return call(kernel, jax.ShapeDtypeStruct((rows, sum(sizes)), bf16), [VM] * len(flat), [], *flat)


def stack_blocks(arrays):
    shape = (len(arrays),) + arrays[0].shape

    def kernel(*refs):
        refs, out, held, sems, out_sems = refs[:-4], refs[-4], refs[-3], refs[-2], refs[-1]
        started, leaving = [], []
        for i, ref in enumerate(refs):
            started.append(pltpu.make_async_copy(ref, held.at[i], sems.at[i]))
            started[-1].start()
        for i, copy in enumerate(started):
            copy.wait()
            leaving.append(pltpu.make_async_copy(held.at[i], out.at[i], out_sems.at[i]))
            leaving[-1].start()
        for copy in leaving:
            copy.wait()

    return pl.pallas_call(
        kernel,
        out_shape=jax.ShapeDtypeStruct(shape, bf16),
        in_specs=[HBM] * len(arrays),
        out_specs=HBM,
        scratch_shapes=[
            pltpu.VMEM(shape, bf16),
            pltpu.SemaphoreType.DMA((len(arrays),)),
            pltpu.SemaphoreType.DMA((len(arrays),)),
        ],
        cost_estimate=pl.CostEstimate(flops=0, bytes_accessed=0, transcendentals=0),
        compiler_params=pltpu.CompilerParams(vmem_limit_bytes=VMEM_LIMIT),
    )(*arrays)


def times_x(where, full, panel, total, half, dtype):
    spots = list(full)
    both, depth = full[spots[0]].shape
    blocks, block, cols = panel.shape
    eighth = block // 8
    count = len(spots)
    extra = [] if total is None else [total]
    part = slice(0, both) if half is None else slice(half * both // 2, (half + 1) * both // 2)
    rows = part.stop - part.start

    def kernel(where_ref, *refs):
        slices, panel_ref, refs = refs[:count], refs[count], refs[count + 1 :]
        out, held, sems = refs[-3:]
        started = []
        for i, spot in enumerate(spots):
            first = pl.multiple_of(place_of(where_ref, *spot) * eighth, eighth)
            copy = pltpu.make_async_copy(panel_ref.at[:, pl.ds(first, eighth)], held.at[i], sems.at[i])
            copy.start()
            started.append(copy)
        for i in range(0, count, 2):
            group = range(i, min(i + 2, count))
            for k in group:
                started[k].wait()
            left = jnp.concatenate([slices[k][part] for k in group], axis=1)
            right = held[i : i + len(group)].reshape(len(group) * depth, cols)
            value = jnp.dot(left, right, preferred_element_type=f32)
            if i > 0:
                value = out[...] + value
            elif extra:
                value = refs[0][part] + value
            out[...] = value.astype(dtype)

    return call(
        kernel, jax.ShapeDtypeStruct((rows, cols), dtype), [SM] + [VM] * count + [HBM] + [VM] * len(extra),
        [pltpu.VMEM((count, blocks, eighth, cols), bf16), pltpu.SemaphoreType.DMA((count,))],
        where, *[full[spot] for spot in spots], panel, *extra,
    )


def add_rounded(mine, got):
    def kernel(m, g, y, v):
        value = m[...] + g[...].astype(f32)
        y[...] = value
        v[...] = value.astype(bf16)

    out = [jax.ShapeDtypeStruct(mine.shape, f32), jax.ShapeDtypeStruct(mine.shape, bf16)]
    return call(kernel, out, [VM] * 2, [], mine, got)


def arrange(where, full):
    spots = list(full)
    both, depth = full[spots[0]].shape
    eighth = depth // 8

    def kernel(where_ref, *refs):
        out, held = refs[8:]
        for spot, part in zip(spots, refs[:8]):
            held[place_of(where_ref, *spot)] = part[...]
        for p in range(8):
            out[p] = jnp.concatenate([held[e, :, p * eighth : (p + 1) * eighth] for e in range(8)], axis=1)

    out = jax.ShapeDtypeStruct((8, both, depth), bf16)
    return call(
        kernel, out, [SM] + [VM] * 8, [pltpu.VMEM((8, both, depth), bf16)], where, *[full[spot] for spot in spots]
    )


def times_y(gram, arrays, first, total, half, dtype):
    _, both, depth = gram.shape
    cols = arrays[0].shape[1]
    copies = [(i, 0, i * depth, depth) for i in range(len(arrays))]
    extra = [] if total is None else [total]
    halves = (0, 1) if half is None else (half,)
    rows = both // 2

    def kernel(gram_ref, *refs):
        ys = refs[len(extra) : len(extra) + len(arrays)]
        out, panel, sems = refs[-3:]
        for copy in start_copies(copies, ys, panel, sems):
            copy.wait()
        for i, one in enumerate(halves):
            part = slice(one * rows, (one + 1) * rows)
            left = jnp.concatenate([gram_ref[first + p, part] for p in range(len(arrays))], axis=1)
            value = jnp.dot(left, panel[...], preferred_element_type=f32)
            if extra:
                value = refs[0][part] + value
            out[i * rows : (i + 1) * rows] = value.astype(dtype)

    return call(
        kernel, jax.ShapeDtypeStruct((rows * len(halves), cols), dtype), [VM] * (1 + len(extra)) + [HBM] * len(arrays),
        [pltpu.VMEM((len(arrays) * depth, cols), bf16), pltpu.SemaphoreType.DMA((len(arrays),))],
        gram, *extra, *arrays,
    )


def result(own, y, mine, got):
    def kernel(own_ref, y_ref, m, g, out):
        square = m[...] + g[...].astype(f32)
        out[...] = (lead_coef * own_ref[...].astype(f32) + square_coef * y_ref[...] + quart_coef * square).astype(bf16)

    return call(kernel, jax.ShapeDtypeStruct(own.shape, bf16), [VM] * 4, [], own, y, mine, got)


def local(own):
    core = lax.axis_index("c")
    where = jnp.stack([lax.axis_index("x"), lax.axis_index("zh"), 1 + 2 * core, 3 - 2 * core]).astype(jnp.int32)
    x = {}

    def terms(keys, send):
        return terms_of(where, own, w, [x[key] for key in keys], send)

    z = swap_zl(own)
    r0 = along_y(own)
    r1 = along_y(own, False)
    w = swap_core(own)
    x[0, "v"] = own
    got0 = partner(terms(OWN, True), True)
    keep0 = terms(OWN, False)
    r0, w, z, r1, got0, keep0 = together(r0, w, z, r1, got0, keep0)
    x[0, "r0"], x[1, "v"], x[0, "r1"] = r0, z, r1
    rz1 = swap_zl(r1)
    rz0 = along_y(z)
    f = along_y(r1, False)
    got1 = partner(terms(EARLY, True), True)
    keep1 = terms(EARLY, False)
    rz0, f, rz1, keep1 = together(rz0, f, rz1, keep1)
    x[0, "f"], x[1, "r0"], x[1, "r1"] = f, rz0, rz1
    fz = along_y(rz0)
    mine1, other1 = sum_pair((keep0, got0), (keep1, got1))
    last1 = partner(other1, False)
    got2 = partner(terms(MIDDLE, True), True)
    keep2 = terms(MIDDLE, False)
    fz, keep2, last1 = together(fz, keep2, last1)
    x[1, "f"] = fz
    got3 = partner(terms(LATE, True), True)
    z1 = swap_zh(sum_other((mine1, last1)))
    keep3 = terms(LATE, False)
    got2, keep3, got3 = together(got2, keep3, got3)
    mine2, other2 = sum_pair((keep2, got2), (keep3, got3))
    last2 = partner(other2, False)
    last2, z1 = together(last2, z1)
    z2 = swap_zh(sum_other((mine2, last2)))
    mine = finish([(mine1, last1), (mine2, last2)], [z1, z2])
    b0 = swap_zh(mine)
    a1 = swap_x1(mine)
    a3 = swap_x3(mine)
    panel = stack_blocks([x[key] for key in ARRIVAL])
    a1, a3, b0, panel = together(a1, a3, b0, panel)
    b3 = swap_x3(b0)
    b1 = swap_x1(b0)
    a2 = swap_x3(a1)
    near = {(0, 0): mine, (1, 0): a1, (3, 0): a3, (0, 1): b0}
    part = times_x(where, near, panel, None, None, f32)
    b1, b3, part = together(b1, b3, part)
    b2 = swap_x1(b3)
    next_ones = {(1, 1): b1, (3, 1): b3}
    part = times_x(where, next_ones, panel, part, None, f32)
    a2, b2, part = together(a2, b2, part)
    late = {(2, 0): a2, (2, 1): b2}
    give = times_x(where, late, panel, part, 1, bf16)
    got = swap_core(give)
    y = times_x(where, late, panel, part, 0, f32)
    got, y = together(got, y)
    y, v = add_rounded(y, got)

    def add(total, keys, half=None, dtype=f32):
        return times_y(gram, [u[key] for key in keys], ARRIVAL.index(keys[0]), total, half, dtype)

    u = {}
    z = swap_zl(v)
    r0 = along_y(v)
    r1 = along_y(v, False)
    gram = arrange(where, near | next_ones | late)
    r0, z, r1, gram = together(r0, z, r1, gram)
    u[0, "v"], u[0, "r0"], u[1, "v"], u[0, "r1"] = v, r0, z, r1
    rz1 = swap_zl(r1)
    rz0 = along_y(z)
    f = along_y(r1, False)
    total = add(None, OWN + EARLY)
    rz0, f, rz1, total = together(rz0, f, rz1, total)
    u[0, "f"], u[1, "r0"], u[1, "r1"] = f, rz0, rz1
    fz = along_y(rz0)
    total = add(total, MIDDLE)
    fz, total = together(fz, total)
    u[1, "f"] = fz
    got = swap_core(add(total, LATE, 1, bf16))
    mine = add(total, LATE, 0)
    got, mine = together(got, mine)
    return result(own, y, mine, got)


def solution(mesh):
    fine = Mesh(mesh.devices.reshape(SIZES), AXES)
    spec = P(ROW, COL)
    return jax.shard_map(local, mesh=fine, in_specs=(spec,), out_specs=spec, check_vma=False)
```

```python
import jax
import jax.numpy as jnp
from jax import lax
from jax.experimental import pallas as pl
from jax.experimental.pallas import tpu as pltpu
from jax.sharding import Mesh, PartitionSpec as P

N = 9216

lead_coef = 3.4445
square_coef = -4.775
quart_coef = 2.0315

AXES = ("zl", "y", "c", "zh", "x")
SIZES = (2, 4, 2, 2, 4)
ROW = ("zl", "y", "c")
COL = ("zh", "x")
f32 = jnp.float32
bf16 = jnp.bfloat16
VMEM_LIMIT = 36 * 2**20

def swap_zl(v):
    return lax.ppermute(v, "zl", [(0, 1), (1, 0)])


def swap_zh(v):
    return lax.ppermute(v, "zh", [(0, 1), (1, 0)])


def swap_core(v):
    return lax.ppermute(v, "c", [(0, 1), (1, 0)])


def swap_x1(v):
    return lax.ppermute(v, "x", [(i, i ^ 1) for i in range(4)])


def swap_x3(v):
    return lax.ppermute(v, "x", [(i, i ^ 3) for i in range(4)])


def partner(v, first):
    pairs = []
    for c in range(2):
        by = 1 if (c == 0) == first else 3
        pairs += [(c * 4 + x, c * 4 + (x ^ by)) for x in range(4)]
    return lax.ppermute(v, ("c", "x"), pairs)


def along_y(v, first=True):
    pairs = []
    for y in range(4):
        for c in range(2):
            by = 1 if (c == 0) == first else -1
            pairs.append((y * 2 + c, (y + by) % 4 * 2 + c))
    return lax.ppermute(v, ("y", "c"), pairs)


def together(*values):
    return lax.optimization_barrier(values)


OWN = ((0, "v"),)
EARLY = ((0, "r0"), (1, "v"), (0, "r1"))
MIDDLE = ((0, "f"), (1, "r0"), (1, "r1"))
LATE = ((1, "f"),)
ARRIVAL = OWN + EARLY + MIDDLE + LATE


VM = pl.BlockSpec(memory_space=pltpu.VMEM)
SM = pl.BlockSpec(memory_space=pltpu.SMEM)
HBM = pl.BlockSpec(memory_space=pltpu.HBM)


def call(kernel, out_shape, in_specs, scratch, *args):
    outs = jax.tree.map(lambda _: VM, out_shape)
    return pl.pallas_call(
        kernel,
        out_shape=out_shape,
        in_specs=in_specs,
        out_specs=outs,
        scratch_shapes=scratch,
        cost_estimate=pl.CostEstimate(flops=0, bytes_accessed=0, transcendentals=0),
        compiler_params=pltpu.CompilerParams(vmem_limit_bytes=VMEM_LIMIT),
    )(*args)


def place_of(where_ref, d, h):
    return jnp.bitwise_xor(where_ref[0], d) * 2 + jnp.bitwise_xor(where_ref[1], h)


def start_copies(copies, refs, panel, sems):
    started = []
    for i, (ref, src, dst, rows) in enumerate(copies):
        copy = pltpu.make_async_copy(refs[ref].at[pl.ds(src, rows)], panel.at[pl.ds(dst, rows)], sems.at[i])
        copy.start()
        started.append(copy)
    return started


def terms_of(where, right, arrays, send):
    rows, depth = arrays[0].shape
    eighth = rows // 8
    count = len(arrays)
    copies = [(i, 0, i * rows, rows) for i in range(count)]

    def kernel(where_ref, right_ref, *refs):
        refs, out, panel, sems = refs[:-3], refs[-3], refs[-2], refs[-1]
        for copy in start_copies(copies, refs, panel, sems):
            copy.wait()
        parts = []
        for d in (where_ref[2], 2) if send else (0, where_ref[3]):
            x = jnp.bitwise_xor(where_ref[0], d)
            for p in range(count):
                first = pl.multiple_of(p * rows + x * 2 * eighth, 2 * eighth)
                parts.append(panel[pl.ds(first, 2 * eighth)])
        left = jnp.concatenate(parts, axis=0)
        value = jnp.dot(left, right_ref[...], preferred_element_type=f32).astype(out.dtype)
        for slot in range(2):
            for p in range(count):
                for z in range(2):
                    first = ((slot * count + p) * 2 + z) * eighth
                    h = jnp.bitwise_xor(where_ref[1], z)
                    out[slot, h, p * eighth : (p + 1) * eighth] = value[first : first + eighth]

    return call(
        kernel, jax.ShapeDtypeStruct((2, 2, count * eighth, 2 * rows), bf16 if send else f32),
        [SM, VM] + [HBM] * count,
        [pltpu.VMEM((count * rows, depth), bf16), pltpu.SemaphoreType.DMA((count,))],
        where, right, *arrays,
    )


def sum_pair(*pairs):
    sizes = [keep.shape[2] for keep, _ in pairs]
    flat = [a for pair in pairs for a in pair]

    def kernel(*refs):
        mine, other = refs[-2:]
        first = 0
        for b, size in enumerate(sizes):
            k, g = refs[2 * b : 2 * b + 2]
            other[:, first : first + size] = (k[1] + g[1].astype(f32)).astype(bf16)
            mine[:, first : first + size] = k[0] + g[0].astype(f32)
            first += size

    shape = (2, sum(sizes), pairs[0][0].shape[3])
    out = [jax.ShapeDtypeStruct(shape, f32), jax.ShapeDtypeStruct(shape, bf16)]
    return call(kernel, out, [VM] * len(flat), [], *flat)


def sum_other(*pairs):
    sizes = [mine.shape[1] for mine, _ in pairs]
    flat = [a for pair in pairs for a in pair]

    def kernel(*refs):
        first = 0
        for b, size in enumerate(sizes):
            refs[-1][first : first + size] = (refs[2 * b][1] + refs[2 * b + 1][1].astype(f32)).astype(bf16)
            first += size

    out = jax.ShapeDtypeStruct((sum(sizes), pairs[0][0].shape[2]), bf16)
    return call(kernel, out, [VM] * len(flat), [], *flat)


def finish(pairs, z_parts):
    sizes = [mine.shape[1] for mine, _ in pairs]
    rows = pairs[0][0].shape[2]
    flat = [a for pair in pairs for a in pair] + z_parts

    def kernel(*refs):
        values = []
        for b in range(len(sizes)):
            values.append(refs[2 * b][0] + refs[2 * b + 1][0].astype(f32))
        value = jnp.concatenate(values, axis=0)
        z_part = jnp.concatenate([ref[...] for ref in refs[2 * len(sizes) : -1]], axis=0)
        refs[-1][...] = ((value + z_part.astype(f32)) / N).T.astype(bf16)

    return call(kernel, jax.ShapeDtypeStruct((rows, sum(sizes)), bf16), [VM] * len(flat), [], *flat)


def stack_blocks(arrays):
    shape = (len(arrays),) + arrays[0].shape

    def kernel(*refs):
        refs, out, held, sems, out_sems = refs[:-4], refs[-4], refs[-3], refs[-2], refs[-1]
        started, leaving = [], []
        for i, ref in enumerate(refs):
            started.append(pltpu.make_async_copy(ref, held.at[i], sems.at[i]))
            started[-1].start()
        for i, copy in enumerate(started):
            copy.wait()
            leaving.append(pltpu.make_async_copy(held.at[i], out.at[i], out_sems.at[i]))
            leaving[-1].start()
        for copy in leaving:
            copy.wait()

    return pl.pallas_call(
        kernel,
        out_shape=jax.ShapeDtypeStruct(shape, bf16),
        in_specs=[HBM] * len(arrays),
        out_specs=HBM,
        scratch_shapes=[
            pltpu.VMEM(shape, bf16),
            pltpu.SemaphoreType.DMA((len(arrays),)),
            pltpu.SemaphoreType.DMA((len(arrays),)),
        ],
        cost_estimate=pl.CostEstimate(flops=0, bytes_accessed=0, transcendentals=0),
        compiler_params=pltpu.CompilerParams(vmem_limit_bytes=VMEM_LIMIT),
    )(*arrays)


def times_x(where, full, panel, total, half, dtype):
    spots = list(full)
    both, depth = full[spots[0]].shape
    blocks, block, cols = panel.shape
    eighth = block // 8
    count = len(spots)
    extra = [] if total is None else [total]
    part = slice(0, both) if half is None else slice(half * both // 2, (half + 1) * both // 2)
    rows = part.stop - part.start

    def kernel(where_ref, *refs):
        slices, panel_ref, refs = refs[:count], refs[count], refs[count + 1 :]
        out, held, sems = refs[-3:]
        started = []
        for i, spot in enumerate(spots):
            first = pl.multiple_of(place_of(where_ref, *spot) * eighth, eighth)
            copy = pltpu.make_async_copy(panel_ref.at[:, pl.ds(first, eighth)], held.at[i], sems.at[i])
            copy.start()
            started.append(copy)
        for i in range(0, count, 2):
            group = range(i, min(i + 2, count))
            for k in group:
                started[k].wait()
            left = jnp.concatenate([slices[k][part] for k in group], axis=1)
            right = held[i : i + len(group)].reshape(len(group) * depth, cols)
            value = jnp.dot(left, right, preferred_element_type=f32)
            if i > 0:
                value = out[...] + value
            elif extra:
                value = refs[0][part] + value
            out[...] = value.astype(dtype)

    return call(
        kernel, jax.ShapeDtypeStruct((rows, cols), dtype), [SM] + [VM] * count + [HBM] + [VM] * len(extra),
        [pltpu.VMEM((count, blocks, eighth, cols), bf16), pltpu.SemaphoreType.DMA((count,))],
        where, *[full[spot] for spot in spots], panel, *extra,
    )


def add_rounded(mine, got):
    def kernel(m, g, y, v):
        value = m[...] + g[...].astype(f32)
        y[...] = value
        v[...] = value.astype(bf16)

    out = [jax.ShapeDtypeStruct(mine.shape, f32), jax.ShapeDtypeStruct(mine.shape, bf16)]
    return call(kernel, out, [VM] * 2, [], mine, got)


def arrange(where, full):
    spots = list(full)
    both, depth = full[spots[0]].shape
    eighth = depth // 8

    def kernel(where_ref, *refs):
        out, held = refs[8:]
        for spot, part in zip(spots, refs[:8]):
            held[place_of(where_ref, *spot)] = part[...]
        for p in range(8):
            out[p] = jnp.concatenate([held[e, :, p * eighth : (p + 1) * eighth] for e in range(8)], axis=1)

    out = jax.ShapeDtypeStruct((8, both, depth), bf16)
    return call(
        kernel, out, [SM] + [VM] * 8, [pltpu.VMEM((8, both, depth), bf16)], where, *[full[spot] for spot in spots]
    )


def times_y(gram, arrays, first, total, half, dtype):
    _, both, depth = gram.shape
    cols = arrays[0].shape[1]
    copies = [(i, 0, i * depth, depth) for i in range(len(arrays))]
    extra = [] if total is None else [total]
    halves = (0, 1) if half is None else (half,)
    rows = both // 2

    def kernel(gram_ref, *refs):
        ys = refs[len(extra) : len(extra) + len(arrays)]
        out, panel, sems = refs[-3:]
        for copy in start_copies(copies, ys, panel, sems):
            copy.wait()
        for i, one in enumerate(halves):
            part = slice(one * rows, (one + 1) * rows)
            left = jnp.concatenate([gram_ref[first + p, part] for p in range(len(arrays))], axis=1)
            value = jnp.dot(left, panel[...], preferred_element_type=f32)
            if extra:
                value = refs[0][part] + value
            out[i * rows : (i + 1) * rows] = value.astype(dtype)

    return call(
        kernel, jax.ShapeDtypeStruct((rows * len(halves), cols), dtype), [VM] * (1 + len(extra)) + [HBM] * len(arrays),
        [pltpu.VMEM((len(arrays) * depth, cols), bf16), pltpu.SemaphoreType.DMA((len(arrays),))],
        gram, *extra, *arrays,
    )


def result(own, y, mine, got):
    def kernel(own_ref, y_ref, m, g, out):
        square = m[...] + g[...].astype(f32)
        out[...] = (lead_coef * own_ref[...].astype(f32) + square_coef * y_ref[...] + quart_coef * square).astype(bf16)

    return call(kernel, jax.ShapeDtypeStruct(own.shape, bf16), [VM] * 4, [], own, y, mine, got)


def local(own):
    core = lax.axis_index("c")
    where = jnp.stack([lax.axis_index("x"), lax.axis_index("zh"), 1 + 2 * core, 3 - 2 * core]).astype(jnp.int32)
    x = {}

    def terms(keys, send):
        return terms_of(where, right, [x[key] for key in keys], send)

    z = swap_zl(own)
    r0 = along_y(own)
    r1 = along_y(own, False)
    w = swap_core(own)
    both = jnp.concatenate(together(own, w), axis=0)
    right = both.T
    x[0, "v"] = own
    got0 = partner(terms(OWN, True), True)
    keep0 = terms(OWN, False)
    r0, w, z, r1, got0, keep0 = together(r0, w, z, r1, got0, keep0)
    x[0, "r0"], x[1, "v"], x[0, "r1"] = r0, z, r1
    rz1 = swap_zl(r1)
    rz0 = along_y(z)
    f = along_y(r1, False)
    got1 = partner(terms(EARLY, True), True)
    keep1 = terms(EARLY, False)
    rz0, f, rz1, keep1 = together(rz0, f, rz1, keep1)
    x[0, "f"], x[1, "r0"], x[1, "r1"] = f, rz0, rz1
    fz = along_y(rz0)
    mine1, other1 = sum_pair((keep0, got0), (keep1, got1))
    last1 = partner(other1, False)
    got2 = partner(terms(MIDDLE, True), True)
    keep2 = terms(MIDDLE, False)
    fz, keep2, last1 = together(fz, keep2, last1)
    x[1, "f"] = fz
    got3 = partner(terms(LATE, True), True)
    z1 = swap_zh(sum_other((mine1, last1)))
    keep3 = terms(LATE, False)
    got2, keep3, got3 = together(got2, keep3, got3)
    mine2, other2 = sum_pair((keep2, got2), (keep3, got3))
    last2 = partner(other2, False)
    last2, z1 = together(last2, z1)
    z2 = swap_zh(sum_other((mine2, last2)))
    mine = finish([(mine1, last1), (mine2, last2)], [z1, z2])
    b0 = swap_zh(mine)
    a1 = swap_x1(mine)
    a3 = swap_x3(mine)
    panel = stack_blocks([x[key] for key in ARRIVAL])
    a1, a3, b0, panel = together(a1, a3, b0, panel)
    b3 = swap_x3(b0)
    b1 = swap_x1(b0)
    a2 = swap_x3(a1)
    near = {(0, 0): mine, (1, 0): a1, (3, 0): a3, (0, 1): b0}
    part = times_x(where, near, panel, None, None, f32)
    b1, b3, part = together(b1, b3, part)
    b2 = swap_x1(b3)
    next_ones = {(1, 1): b1, (3, 1): b3}
    part = times_x(where, next_ones, panel, part, None, f32)
    a2, b2, part = together(a2, b2, part)
    late = {(2, 0): a2, (2, 1): b2}
    give = times_x(where, late, panel, part, 1, bf16)
    got = swap_core(give)
    y = times_x(where, late, panel, part, 0, f32)
    got, y = together(got, y)
    y, v = add_rounded(y, got)

    def add(total, keys, half=None, dtype=f32):
        return times_y(gram, [u[key] for key in keys], ARRIVAL.index(keys[0]), total, half, dtype)

    u = {}
    z = swap_zl(v)
    r0 = along_y(v)
    r1 = along_y(v, False)
    gram = arrange(where, near | next_ones | late)
    r0, z, r1, gram = together(r0, z, r1, gram)
    u[0, "v"], u[0, "r0"], u[1, "v"], u[0, "r1"] = v, r0, z, r1
    rz1 = swap_zl(r1)
    rz0 = along_y(z)
    f = along_y(r1, False)
    total = add(None, OWN + EARLY)
    rz0, f, rz1, total = together(rz0, f, rz1, total)
    u[0, "f"], u[1, "r0"], u[1, "r1"] = f, rz0, rz1
    fz = along_y(rz0)
    total = add(total, MIDDLE)
    fz, total = together(fz, total)
    u[1, "f"] = fz
    got = swap_core(add(total, LATE, 1, bf16))
    mine = add(total, LATE, 0)
    got, mine = together(got, mine)
    return result(own, y, mine, got)


def solution(mesh):
    fine = Mesh(mesh.devices.reshape(SIZES), AXES)
    spec = P(ROW, COL)
    return jax.shard_map(local, mesh=fine, in_specs=(spec,), out_specs=spec, check_vma=False)
```
